32 devices in a mesh: dp: 16 (over z, x, core), tensor: 2 (over y).
Axes of the slice: x: 2, y: 2, z: 4, core: 2. Of those that a mesh axis runs over, the one named last changes fastest.
Arguments:
- tokens: bfloat16 [16384, 1024], P(('dp', 'tensor')), may hold values from -6 to 6
- cond: bfloat16 [16, 1024], P('dp'), may hold values from -6 to 6
- ada_w: bfloat16 [1024, 6, 1024], P('dp', None, 'tensor'), may hold values from -0.1875 to 0.1875
- ada_b: bfloat16 [6, 16, 64], P(None, 'tensor', 'dp'), may hold values from -3 to 3
- qkv_w: bfloat16 [1024, 3, 1024], P('dp', None, 'tensor'), may hold values from -0.1875 to 0.1875
- qv_b: bfloat16 [2, 16, 64], P(None, 'tensor', 'dp'), may hold values from -3 to 3
- proj_w: bfloat16 [1024, 1024], P('tensor', 'dp'), may hold values from -3 to 3
- proj_b: bfloat16 [1024], P('dp'), may hold values from -3 to 3
- fc1_w: bfloat16 [1024, 4096], P('dp', 'tensor'), may hold values from -0.1875 to 0.1875
- fc1_b: bfloat16 [64, 64], P('tensor', 'dp'), may hold values from -3 to 3
- fc2_w: bfloat16 [4096, 1024], P('tensor', 'dp'), may hold values from -0.09375 to 0.09375
- fc2_b: bfloat16 [1024], P('dp'), may hold values from -3 to 3
- grad_out: bfloat16 [16384, 1024], P(('dp', 'tensor')), may hold values from -6 to 6
Outputs:
- block_out: bfloat16 [16384, 1024], P(('dp', 'tensor'))
- grad_tokens: bfloat16 [16384, 1024], P(('dp', 'tensor'))
- grad_cond: bfloat16 [16, 1024], P('dp')
- grad_ada_w: float32 [1024, 6, 1024], P('dp', None, 'tensor')
- grad_ada_b: float32 [6, 16, 64], P(None, 'tensor', 'dp')
- grad_qkv_w: float32 [1024, 3, 1024], P('dp', None, 'tensor')
- grad_qv_b: float32 [2, 16, 64], P(None, 'tensor', 'dp')
- grad_proj_w: float32 [1024, 1024], P('tensor', 'dp')
- grad_proj_b: float32 [1024], P('dp')
- grad_fc1_w: float32 [1024, 4096], P('dp', 'tensor')
- grad_fc1_b: float32 [64, 64], P('tensor', 'dp')
- grad_fc2_w: float32 [4096, 1024], P('tensor', 'dp')
- grad_fc2_b: float32 [1024], P('dp')
The draws below stay inside these ranges and needn't reach their ends.
All inputs are finite; a program needn't handle non-finite values.
Results may differ from the reference program's by a relative error of at most 0.02.
The reference program's roundings to bfloat16 on the way count: a program that leaves them out, or rounds other values in their place, can miss the bound.
Values may be sent and summed in bfloat16 or wider, within the bound.
No kernel may reach another device: no remote copies, remote signals or barrier semaphores. Data moves between devices by JAX's collectives and lax.ppermute only.
A program may use at most 256 MiB of HBM per device.

```python
import jax
import jax.numpy as jnp
from jax import lax

D = 1024
HEADS = 16
HEAD_DIM = 64
FF = 4096
SEQ = 1024
LATENTS = 16
TOKENS = 16384


def raised(array, rng, source, target, parts, factor):
    owner, partner = [(jnp.arange(array.shape[axis_at]) // (array.shape[axis_at] // parts)).reshape([-1 if axis == axis_at else 1 for axis in range(array.ndim)]) for axis_at in (source, target)]
    chosen = jax.random.permutation(rng, parts)[partner]
    strong = (owner == chosen) | (owner == (partner + parts // 2) % parts)
    return jnp.where(strong, factor * array, array)


def shard_levels(rng, shape, cuts, smallest, top_value):
    def one(axis_at, shards_of):
        heights = jax.random.uniform(jax.random.fold_in(jax.random.fold_in(rng, 6), axis_at), (shards_of,), jnp.float32, smallest / len(cuts), top_value / len(cuts))
        return jnp.repeat(jnp.exp(heights), shape[axis_at] // shards_of).reshape((-1,) + (1,) * (len(shape) - axis_at - 1))

    gain = one(*cuts[0])
    for cut in cuts[1:]:
        gain = gain * one(*cut)
    return gain


def gaussian(key, extent, deviation, reach, cuts=(), dtype=jnp.bfloat16):
    level = shard_levels(key, extent, cuts, -0.22, 0.18) if cuts else 1.0
    values = jax.random.normal(key, extent, jnp.float32) * deviation * level
    return jnp.minimum(jnp.maximum(values, -reach), reach).astype(dtype)


def noise_with(key, shape, deviation, bound, cuts, heavy, kind=jnp.bfloat16):
    entries = deviation * jax.random.normal(key, shape, jnp.float32)
    if cuts:
        entries = entries * shard_levels(key, shape, cuts, -0.22, 0.18)
    return jnp.clip(raised(entries, jax.random.fold_in(key, 3), *heavy), -bound, bound).astype(kind)


def setup_inputs(seed: int = 0) -> dict:
    keys = jax.random.split(jax.random.key(seed), 14)
    tokens = gaussian(keys[0], (TOKENS, D), 1.0, 6.0, ((0, 32),))
    cond = gaussian(keys[1], (LATENTS, D), 1.0, 6.0, ((0, 16),))
    ada_w = gaussian(keys[2], (D, 6, D), D ** -0.5, 0.1875, ((0, 16), (2, 2)))
    ada_b = gaussian(keys[3], (6, HEADS, HEAD_DIM), 0.5, 3.0, ((1, 2), (2, 16)))
    qkv_w = gaussian(keys[4], (D, 3, D), D ** -0.5, 0.1875, ((0, 16), (2, 2)))
    qv_b = gaussian(keys[5], (2, HEADS, HEAD_DIM), 0.5, 3.0, ((1, 2), (2, 16)))
    proj_w = gaussian(keys[6], (D, D), (4 * D // SEQ) ** -0.5, 3.0, ((0, 2), (1, 16)))
    proj_b = gaussian(keys[7], (D,), 0.5, 3.0, ((0, 16),))
    fc1_w = gaussian(keys[8], (D, FF), D ** -0.5, 0.1875, ((0, 16), (1, 2)))
    fc1_b = gaussian(keys[9], (FF // HEAD_DIM, HEAD_DIM), 0.5, 3.0, ((0, 2), (1, 16)))
    fc2_w = gaussian(keys[10], (FF, D), FF ** -0.5, 0.09375, ((0, 2), (1, 16)))
    fc2_b = gaussian(keys[11], (D,), 0.5, 3.0, ((0, 16),))
    grad_out = noise_with(keys[12], (TOKENS, D), 1.0, 6.0, ((0, 32),), (0, 1, 32, 2.75))
    return dict(tokens=tokens, cond=cond, ada_w=ada_w, ada_b=ada_b, qkv_w=qkv_w, qv_b=qv_b, proj_w=proj_w, proj_b=proj_b, fc1_w=fc1_w, fc1_b=fc1_b, fc2_w=fc2_w, fc2_b=fc2_b, grad_out=grad_out)


eps_norm = 1e-06

@jax.custom_vjp
def low(v):
    return lax.optimization_barrier(v.astype(jnp.bfloat16)).astype(jnp.float32)

@jax.custom_vjp
def low_back(v):
    return v

def low_keep(v):
    return (low(v), None)

def low_pass(kept, grad):
    return (grad,)

def back_keep(v):
    return (v, None)

def back_low(kept, grad):
    return (low(grad),)
low.defvjp(low_keep, low_pass)
low_back.defvjp(back_keep, back_low)

def layer_norm(values):
    centre = values - lax.optimization_barrier(jnp.mean(values, axis=-1, keepdims=True))
    return centre * lax.rsqrt(lax.optimization_barrier(jnp.mean(centre * centre, axis=-1, keepdims=True)) + eps_norm)

def latent_layer(tokens_one, mod_one, weights):
    qkv_w, qv_b, proj_w, proj_b, fc1_w, fc1_b, fc2_w, fc2_b = weights
    highest = lax.Precision.HIGHEST
    attn_in = low(layer_norm(tokens_one) * (1.0 + mod_one[1]) + mod_one[0])
    projected = jnp.einsum('td,dke->tke', attn_in, qkv_w, precision=highest)
    biases = qv_b.reshape(2, D)
    queries = low(low_back(projected[:, 0] + biases[0]))
    key_rows = low(low_back(projected[:, 1]))
    value_rows = low(low_back(projected[:, 2] + biases[1]))
    head_shape = (SEQ, HEADS, HEAD_DIM)
    scores = jnp.einsum('qhe,khe->hqk', queries.reshape(head_shape), key_rows.reshape(head_shape), precision=highest)
    scores = low_back(scores * HEAD_DIM ** (-0.5))
    row_max = lax.optimization_barrier(jnp.max(scores, axis=-1, keepdims=True))
    exponents = jnp.exp(scores - row_max)
    probs = low(exponents / lax.optimization_barrier(jnp.sum(exponents, axis=-1, keepdims=True)))
    attended = jnp.einsum('hqk,khe->qhe', probs, value_rows.reshape(head_shape), precision=highest).reshape(SEQ, D)
    attended = low(low_back(attended))
    branch_one = low_back(jnp.dot(attended, proj_w, precision=highest) + proj_b)
    residual_mid = tokens_one + mod_one[2] * branch_one
    mlp_in = low(layer_norm(residual_mid) * (1.0 + mod_one[4]) + mod_one[3])
    hidden = low_back(jnp.dot(mlp_in, fc1_w, precision=highest) + fc1_b.reshape(FF))
    active = low(jax.nn.gelu(hidden, approximate=True))
    branch_two = low_back(jnp.dot(active, fc2_w, precision=highest) + fc2_b)
    return residual_mid + mod_one[5] * branch_two

def forward(tokens, cond, ada_w, ada_b, qkv_w, qv_b, proj_w, proj_b, fc1_w, fc1_b, fc2_w, fc2_b):
    silu_low = low(jax.nn.silu(cond))
    modulation = jnp.einsum('ld,dke->lke', silu_low, ada_w, precision=lax.Precision.HIGHEST) + ada_b.reshape(6, D)
    modulation = low_back(modulation)
    weights = (qkv_w, qv_b, proj_w, proj_b, fc1_w, fc1_b, fc2_w, fc2_b)

    def latent_step(latent_items):
        return latent_layer(latent_items[0], latent_items[1], weights)
    outputs = lax.map(jax.checkpoint(latent_step), (tokens.reshape(LATENTS, SEQ, D), modulation))
    return outputs.reshape(TOKENS, D)

def reference(tokens, cond, ada_w, ada_b, qkv_w, qv_b, proj_w, proj_b, fc1_w, fc1_b, fc2_w, fc2_b, grad_out):
    primals = tuple((operand.astype(jnp.float32) for operand in (tokens, cond, ada_w, ada_b, qkv_w, qv_b, proj_w, proj_b, fc1_w, fc1_b, fc2_w, fc2_b)))
    result, pullback = jax.vjp(forward, *primals)
    gradients = pullback(grad_out.astype(jnp.float32))
    return (result.astype(jnp.bfloat16), gradients[0].astype(jnp.bfloat16), gradients[1].astype(jnp.bfloat16), gradients[2], gradients[3], gradients[4], gradients[5], gradients[6], gradients[7], gradients[8], gradients[9], gradients[10], gradients[11])
```

```python
import functools

import jax
import jax.numpy as jnp
from jax import lax
from jax.experimental import pallas as pl
from jax.experimental.pallas import tpu as pltpu
from jax.sharding import PartitionSpec as P

eps_norm = 1e-06
log2_e = 1.4426950408889634
both_axes = ("dp", "tensor")
f32 = jnp.float32
bf16 = jnp.bfloat16


def normalize(values):
    centre = values - jnp.mean(values, axis=-1, keepdims=True)
    inverse = lax.rsqrt(jnp.mean(centre * centre, axis=-1, keepdims=True) + eps_norm)
    return (centre * inverse, inverse)


def norm_back(grad_normed, normed, inverse):
    first = jnp.mean(grad_normed, axis=-1, keepdims=True)
    second = jnp.mean(grad_normed * normed, axis=-1, keepdims=True)
    return inverse * (grad_normed - first - normed * second)


def gelu_tanh(values):
    return jax.nn.gelu(values, approximate=True)


def dot_rows(left, right):
    return lax.dot_general(left, right, (((1,), (0,)), ((), ())), preferred_element_type=f32)


def dot_last(left, right):
    return lax.dot_general(left, right, (((1,), (1,)), ((), ())), preferred_element_type=f32)


def dot_first(left, right):
    return lax.dot_general(left, right, (((0,), (0,)), ((), ())), preferred_element_type=f32)


def head_masks(lanes, head_size):
    lane = lax.broadcasted_iota(jnp.int32, (1, lanes), 1)
    return [
        (lane >= h * head_size) & (lane < (h + 1) * head_size) for h in range(lanes // head_size)
    ]


def attend_kernel(head_size, q_ref, k_ref, v_ref, out_ref):
    lanes = q_ref.shape[1]
    masks = head_masks(lanes, head_size)
    factor = head_size**-0.5 * log2_e
    queries = q_ref[...]
    keys = k_ref[...]
    values = v_ref[...]
    result = None
    for mask in masks:
        scores = dot_last(jnp.where(mask, queries, jnp.zeros_like(queries)), keys)
        top = jnp.max(scores, axis=1, keepdims=True)
        powers = jnp.exp2((scores - top) * factor)
        total = jnp.sum(powers, axis=1, keepdims=True)
        part = dot_rows(powers.astype(bf16), values) * (1.0 / total)
        result = part if result is None else jnp.where(mask, part, result)
    out_ref[...] = result.astype(bf16)


def attend_back_kernel(head_size, q_ref, k_ref, v_ref, g_ref, *refs):
    out_ref, sum_k, sum_v = refs[-3:]
    lanes = q_ref.shape[1]
    masks = head_masks(lanes, head_size)
    scale = head_size**-0.5
    factor = scale * log2_e
    step = pl.program_id(1)

    @pl.when(step == 0)
    def _():
        queries = q_ref[...]
        grads = g_ref[...]
        keys = k_ref[...]
        values = v_ref[...]
        zero = jnp.zeros_like(keys)
        result = None
        for h, mask in enumerate(masks):
            scores = dot_last(jnp.where(mask, keys, zero), queries)
            top = jnp.max(scores, axis=0, keepdims=True)
            powers = jnp.exp2((scores - top) * factor)
            probs = powers * (1.0 / jnp.sum(powers, axis=0, keepdims=True))
            grad_probs = dot_last(jnp.where(mask, values, zero), grads)
            inner = jnp.sum(probs * grad_probs, axis=0, keepdims=True)
            grad_scores = (probs * (grad_probs - inner)).astype(bf16)
            sum_v[h] = dot_rows(probs.astype(bf16), grads)
            sum_k[h] = dot_rows(grad_scores, queries)
            part = dot_first(grad_scores, keys)
            result = part if result is None else jnp.where(mask, part, result)
        out_ref[...] = (result * scale).astype(bf16)

    def joined(sums):
        total = sums[0]
        for h in range(1, len(masks)):
            total = jnp.where(masks[h], sums[h], total)
        return total

    @pl.when(step == 1)
    def _():
        out_ref[...] = (joined(sum_k) * scale).astype(bf16)

    @pl.when(step == 2)
    def _():
        out_ref[...] = joined(sum_v).astype(bf16)


def column_spec(rows, lanes, first, row_block=0):
    return pl.BlockSpec((rows, lanes), lambda j: (row_block, first + j))


def attention(projected, row_block, row_blocks, part_width, head_size):
    rows = projected.shape[0]
    here = rows // row_blocks
    lanes = min(128, part_width)
    count = part_width // lanes
    work = rows * here * part_width
    return pl.pallas_call(
        functools.partial(attend_kernel, head_size),
        out_shape=jax.ShapeDtypeStruct((here, part_width), bf16),
        grid=(count,),
        in_specs=[
            column_spec(here, lanes, 0, row_block),
            column_spec(rows, lanes, count),
            column_spec(rows, lanes, 2 * count),
        ],
        out_specs=column_spec(here, lanes, 0),
        compiler_params=pltpu.CompilerParams(vmem_limit_bytes=40 * 1024 * 1024),
        cost_estimate=pl.CostEstimate(
            flops=16 * work,
            bytes_accessed=8 * rows * part_width,
            transcendentals=work // head_size,
        ),
    )(projected, projected, projected)


def attention_back(projected, grads, earlier, first, blocks, part_width, head_size):
    rows = projected.shape[0]
    lanes = min(128, part_width)
    count = part_width // lanes
    work = rows * rows * blocks * lanes
    sums = pltpu.VMEM((lanes // head_size, rows, lanes), f32)

    def items(part):
        return pl.BlockSpec((rows, lanes), lambda j, p: (0, part * count + first + j))

    in_specs = [items(0), items(1), items(2), items(0)]
    operands = [projected, projected, projected, grads]
    aliases = {}
    if earlier is not None:
        in_specs.append(pl.BlockSpec(memory_space=pl.ANY))
        operands.append(earlier)
        aliases = {4: 0}
    return pl.pallas_call(
        functools.partial(attend_back_kernel, head_size),
        out_shape=jax.ShapeDtypeStruct((rows, 3 * part_width), bf16),
        grid=(blocks, 3),
        in_specs=in_specs,
        out_specs=pl.BlockSpec((rows, lanes), lambda j, p: (0, p * count + first + j)),
        scratch_shapes=[sums, sums],
        input_output_aliases=aliases,
        compiler_params=pltpu.CompilerParams(vmem_limit_bytes=48 * 1024 * 1024),
        cost_estimate=pl.CostEstimate(
            flops=40 * work,
            bytes_accessed=14 * rows * blocks * lanes,
            transcendentals=work // head_size,
        ),
    )(*operands)


def finish_kernel(resid_ref, own_ref, other_ref, bias_ref, gate_ref, grad_ref, out_ref, sum_ref):
    branch = own_ref[...] + other_ref[...].astype(f32) + bias_ref[...]
    out_ref[...] = (resid_ref[...] + gate_ref[...] * branch).astype(bf16)

    @pl.when(pl.program_id(0) == 0)
    def _():
        sum_ref[...] = jnp.zeros_like(sum_ref)

    sum_ref[...] += jnp.sum(grad_ref[...].astype(f32) * branch, axis=0, keepdims=True)


def finish(resid, own, other, bias, gate, grads):
    rows, width = resid.shape
    block = min(128, rows)
    many = pl.BlockSpec((block, width), lambda i: (i, 0))
    single = pl.BlockSpec((1, width), lambda i: (0, 0))
    return pl.pallas_call(
        finish_kernel,
        out_shape=(
            jax.ShapeDtypeStruct((rows, width), bf16),
            jax.ShapeDtypeStruct((1, width), f32),
        ),
        grid=(rows // block,),
        in_specs=[many, many, many, single, single, many],
        out_specs=(many, single),
        compiler_params=pltpu.CompilerParams(vmem_limit_bytes=24 * 1024 * 1024),
        cost_estimate=pl.CostEstimate(
            flops=6 * rows * width, bytes_accessed=14 * rows * width, transcendentals=0
        ),
    )(resid, own, other, bias, gate, grads)


class PairPlan:
    def __init__(self, dp_size):
        self.dp_size = dp_size
        self.index = lax.axis_index("dp")
        self.masks = [1 << b for b in range(dp_size.bit_length() - 1)]
        self.blocks = 2

    def tie(self, values, *others):
        return lax.optimization_barrier((values,) + others)[0]

    def across(self, values):
        return lax.ppermute(values, "tensor", [(0, 1), (1, 0)])

    def swap(self, values, mask):
        return lax.ppermute(values, "dp", [(i, i ^ mask) for i in range(self.dp_size)])

    def upper(self, mask):
        return (self.index // mask) % 2 == 1

    def join(self, own, other, upper, axis):
        return jnp.stack([jnp.where(upper, other, own), jnp.where(upper, own, other)], axis=axis)

    def gather_dp(self, values):
        gathered = values
        for mask in self.masks:
            gathered = self.join(gathered, self.swap(gathered, mask), self.upper(mask), 0)
        return gathered.reshape((-1,) + values.shape)

    def reduce_dp(self, values, order, stages=None):
        shape = values.shape[1:]
        bits = self.masks[::-1]
        values = values.reshape((2,) * len(bits) + shape)
        for mask in order:
            axis = bits.index(mask)
            bits.remove(mask)
            upper = self.upper(mask)
            low = lax.index_in_dim(values, 0, axis, keepdims=False)
            high = lax.index_in_dim(values, 1, axis, keepdims=False)
            received = self.swap(jnp.where(upper, low, high), mask)
            own = jnp.where(upper, high, low)
            values = (own.astype(f32) + received.astype(f32)).astype(values.dtype)
            if stages is not None:
                stages.append(values)
        return values

    def scatter_last(self, grads, stages):
        values = grads.reshape(self.dp_size, -1, grads.shape[1])
        return self.reduce_dp(values, self.masks, stages)

    def send(self, rows):
        return self.across(rows)

    def gather(self, rows, received):
        return [rows, received]

    def scatter(self, term):
        sent = term(1, None).astype(bf16)
        received = self.across(sent)
        return term(0, sent), received

    def total(self, own, received):
        return own + received.astype(f32)

    def join_columns(self, own, received):
        second = lax.axis_index("tensor") == 1
        return jnp.concatenate(
            [jnp.where(second, received, own), jnp.where(second, own, received)], axis=-1
        )

    def split_columns(self, values):
        half = values.shape[-1] // 2
        second = lax.axis_index("tensor") == 1
        low = values[..., :half]
        high = values[..., half:]
        return jnp.where(second, high, low), jnp.where(second, low, high)

    def columns(self, values):
        return self.join(values, self.across(values), lax.axis_index("tensor") == 1, 1).reshape(
            values.shape[0], -1
        )

    def scatter_columns(self, values):
        split = values.reshape(values.shape[0], 2, -1)
        second = lax.axis_index("tensor") == 1
        own = jnp.where(second, split[:, 1], split[:, 0])
        other = jnp.where(second, split[:, 0], split[:, 1])
        return own + self.across(other)

    def sum_tensor(self, values):
        return values + self.across(values)


class AxisPlan:
    def __init__(self):
        self.blocks = 1

    def tie(self, values, *others):
        return values

    def gather_dp(self, values):
        return lax.all_gather(values, "dp", axis=0)

    def reduce_dp(self, values, order):
        return lax.psum_scatter(values, "dp", scatter_dimension=0, tiled=False)

    def scatter_last(self, grads, stages):
        return lax.psum_scatter(grads, "dp", scatter_dimension=0, tiled=True)

    def send(self, rows):
        return rows

    def gather(self, rows, received):
        return [lax.all_gather(rows, "tensor", axis=0, tiled=True)]

    def scatter(self, term):
        return (
            lax.psum_scatter(term(0, None).astype(bf16), "tensor", scatter_dimension=0, tiled=True),
            None,
        )

    def total(self, own, received):
        return own.astype(f32)

    def columns(self, values):
        return lax.all_gather(values, "tensor", axis=1, tiled=True)

    def scatter_columns(self, values):
        return lax.psum_scatter(values, "tensor", scatter_dimension=1, tiled=True)

    def sum_tensor(self, values):
        return lax.psum(values, "tensor")


def stack_rows(blocks):
    return blocks[0] if len(blocks) == 1 else jnp.concatenate(blocks, axis=0)


def body(
    dp_size,
    parts,
    tokens,
    cond,
    ada_w,
    ada_b,
    qkv_w,
    qv_b,
    proj_w,
    proj_b,
    fc1_w,
    fc1_b,
    fc2_w,
    fc2_b,
    grad_out,
):
    paired = parts == 2 and dp_size == 1 << (dp_size.bit_length() - 1)
    plan = PairPlan(dp_size) if paired else AxisPlan()
    dp_index = lax.axis_index("dp")
    width = tokens.shape[1]
    shard = ada_w.shape[0]
    part_width = qkv_w.shape[2]
    hidden_part = fc1_w.shape[1]
    heads_part = qv_b.shape[1]
    piece = qv_b.shape[2]
    head_size = piece * dp_size
    qkv_width = 3 * part_width
    extra = 128
    assert cond.shape[0] == 1

    biases = jnp.concatenate([v.reshape(-1) for v in (qv_b, fc1_b, proj_b, fc2_b)])
    bias_count = biases.shape[0]
    assert bias_count <= shard * extra
    biases = jnp.pad(biases, (0, shard * extra - bias_count)).reshape(shard, extra)
    proj_shard = proj_w.T
    if paired:
        proj_shard = plan.join_columns(proj_shard, plan.send(proj_shard))
    proj_width = proj_shard.shape[1]
    first_shard = jnp.concatenate([qkv_w.reshape(shard, qkv_width), biases, proj_shard], axis=1)

    def gather_weight(values):
        return lax.all_gather(values, "dp", axis=0, tiled=True)

    def scatter_weight(values):
        return lax.psum_scatter(values, "dp", scatter_dimension=1, tiled=True)

    first_full = gather_weight(first_shard)
    tokens_all = plan.gather(tokens, plan.send(tokens))
    grad_out_sent = plan.send(plan.tie(grad_out, tokens_all[-1]))

    small = plan.gather_dp(jnp.concatenate([cond.reshape(-1), ada_b.reshape(-1)]))
    mlp_shard = jnp.stack([fc1_w, fc2_w.T])
    mlp_full = lax.all_gather(plan.tie(mlp_shard, small), "dp", axis=1, tiled=True)
    fc1_full = mlp_full[0]
    fc2_full = mlp_full[1]
    cond_all = small[:, :width].astype(f32)
    ada_bias = small[:, width:].reshape(dp_size, 6, heads_part, piece)
    ada_bias = ada_bias.transpose(1, 2, 0, 3).reshape(6, part_width).astype(f32)
    silu_all = jax.nn.silu(cond_all).astype(bf16)
    silu_own = lax.dynamic_slice_in_dim(silu_all, dp_index * shard, shard, axis=1)
    mod_terms = jnp.einsum("ld,dke->lke", silu_own, ada_w, preferred_element_type=f32)
    order = plan.masks[::-1] if paired else ()
    mod_part = plan.tie(plan.reduce_dp(mod_terms, order) + ada_bias, tokens_all[-1])
    modulation = plan.columns(mod_part)
    shift_one, scale_one, gate_one, shift_two, scale_two, gate_two = [
        modulation[k : k + 1] for k in range(6)
    ]

    attn_blocks = []
    for rows in tokens_all:
        normed, inverse = normalize(rows.astype(f32))
        attn_blocks.append((normed * (1.0 + scale_one) + shift_one).astype(bf16))
        if len(attn_blocks) == 1:
            normed_one, inverse_one = normed, inverse
    residual_in = tokens.astype(f32)
    if not paired:
        normed_one, inverse_one = normalize(residual_in)
    qkv_full = first_full[:, :qkv_width]
    proj_full = first_full[:, qkv_width + extra :]
    biases = first_full[:, qkv_width : qkv_width + extra].reshape(dp_size, -1)[:, :bias_count].astype(f32)
    start = qv_b.size + fc1_b.size
    head_bias = biases[:, :start].reshape(dp_size, -1, piece).transpose(1, 0, 2).reshape(-1)
    qv_bias = head_bias[: 2 * part_width].reshape(2, part_width)
    fc1_bias = head_bias[2 * part_width :]
    proj_bias = biases[:, start : start + shard].reshape(width)
    fc2_bias = biases[:, start + shard :].reshape(width)
    qkv_bias = jnp.concatenate([qv_bias[0], jnp.zeros((part_width,), f32), qv_bias[1]])
    attn_all = stack_rows(attn_blocks)
    projected = (dot_rows(attn_all, qkv_full) + qkv_bias).astype(bf16)

    grad_top = grad_out.astype(f32)
    grad_two = [
        (gate_two * rows.astype(f32)).astype(bf16) for rows in plan.gather(grad_out, grad_out_sent)
    ]
    grad_two_all = stack_rows(grad_two)
    attended = [None] * plan.blocks

    def rows_of(values, block):
        count = values.shape[0] // plan.blocks
        return values[block * count : (block + 1) * count]

    def attend(block, items):
        return attention(items, block, plan.blocks, part_width, head_size)

    def attend_term(block, earlier):
        attended[block] = attend(block, projected)
        return dot_last(attended[block], proj_full)

    if paired:
        attended_sent = plan.send(attend(1, projected))
        attended_own = attend(0, plan.tie(projected, grad_out_sent))
        attended_own = plan.join_columns(attended_own, attended_sent)
        branch_one = dot_last(attended_own, proj_full) + proj_bias
    else:
        branch_one = plan.total(*plan.scatter(attend_term)) + proj_bias
    residual_mid = residual_in + gate_one * branch_one
    normed_two, inverse_two = normalize(residual_mid)
    mlp_low = (normed_two * (1.0 + scale_two) + shift_two).astype(bf16)
    mlp_blocks = plan.gather(mlp_low, plan.send(mlp_low))
    mlp_all = stack_rows(mlp_blocks)
    hidden = [dot_rows(rows, fc1_full) + fc1_bias for rows in mlp_blocks]
    active_blocks = [gelu_tanh(rows).astype(bf16) for rows in hidden]
    active = stack_rows(active_blocks)

    grad_hidden = [None] * plan.blocks

    def mlp_back_term(block, earlier):
        grads = grad_two[block] if earlier is None else plan.tie(grad_two[block], earlier)
        pull = jax.vjp(gelu_tanh, hidden[block])[1]
        grad_hidden[block] = pull(dot_rows(grads, fc2_full))[0].astype(bf16)
        return dot_last(grad_hidden[block], fc1_full)

    grad_mlp_own, grad_mlp_sent = plan.scatter(mlp_back_term)
    grad_hidden_all = stack_rows(grad_hidden)
    mlp_sums = lax.dot_general(
        jnp.stack([mlp_all, grad_two_all]),
        jnp.stack([grad_hidden_all, active]),
        (((1,), (1,)), ((0,), (0,))),
        preferred_element_type=f32,
    ).astype(bf16)
    second_sum = lax.psum_scatter(mlp_sums, "dp", scatter_dimension=1, tiled=True)
    grad_mlp_own = plan.tie(grad_mlp_own, mlp_sums)
    grad_mlp_in = plan.total(grad_mlp_own, grad_mlp_sent)
    grad_resid = grad_top + norm_back(grad_mlp_in * (1.0 + scale_two), normed_two, inverse_two)
    grad_branch_one = (gate_one * grad_resid).astype(bf16)
    proj_sum = jnp.sum(grad_branch_one, axis=0, dtype=f32)
    grad_proj_sent = None
    if paired:
        near_proj, far_proj = plan.split_columns(proj_full)
        grad_attended = dot_rows(grad_branch_one, far_proj).astype(bf16)
        grad_attended_sent = plan.send(grad_attended)
        grad_attended = dot_rows(grad_branch_one, near_proj).astype(bf16)
        near_attended, far_attended = plan.split_columns(attended_own)
        far_proj_sum = dot_first(grad_branch_one, far_attended).astype(bf16)
        grad_proj = dot_first(grad_branch_one, near_attended)
        grad_attended_sent = plan.tie(grad_attended_sent, far_proj_sum, grad_proj)
        grad_proj_sent = plan.send(plan.tie(far_proj_sum, grad_attended_sent))
        proj_sum = plan.sum_tensor(plan.tie(proj_sum, grad_attended_sent))
        grad_attended = stack_rows([grad_attended, grad_attended_sent])
    else:
        grad_one_all = stack_rows(plan.gather(grad_branch_one, plan.send(grad_branch_one)))
        proj_sum = jnp.sum(grad_one_all, axis=0, dtype=f32)
        grad_proj = dot_first(grad_one_all, stack_rows(attended)).astype(bf16)
        grad_attended = dot_rows(grad_one_all, proj_full).astype(bf16)

    def mlp_term(block, earlier):
        items = active_blocks[block]
        if block == plan.blocks - 1:
            items = plan.tie(items, grad_attended)
        return dot_last(items, fc2_full)

    branch_two_parts = plan.scatter(mlp_term)
    lane_blocks = part_width // min(128, part_width)
    calls = 2 if lane_blocks % 2 == 0 else 1
    grad_projected = None
    for call in range(calls):
        if call == 1:
            grad_attended = plan.tie(grad_attended, grad_proj_sent, proj_sum)
        grad_projected = attention_back(
            projected,
            grad_attended,
            grad_projected,
            call * (lane_blocks // calls),
            lane_blocks // calls,
            part_width,
            head_size,
        )

    def attn_back_term(block, earlier):
        items = rows_of(grad_projected, block)
        if earlier is not None:
            items = plan.tie(items, earlier)
        return dot_last(items, qkv_full)

    grad_attn_own, grad_attn_sent = plan.scatter(attn_back_term)


    def token_sum(values):
        return jnp.sum(values, axis=0, dtype=f32)

    qkv_sums = token_sum(grad_projected)
    head_sums = jnp.concatenate(
        [qkv_sums[:part_width], qkv_sums[2 * part_width :], token_sum(grad_hidden_all)]
    )
    head_sums = head_sums.reshape(-1, dp_size, piece).transpose(1, 0, 2).reshape(dp_size, -1)
    bias_sums = jnp.concatenate(
        [
            head_sums,
            proj_sum.reshape(dp_size, shard),
            token_sum(grad_two_all).reshape(dp_size, shard),
        ],
        axis=1,
    ).astype(bf16)
    bias_sums = jnp.pad(bias_sums, ((0, 0), (0, shard * extra - bias_count)))
    first_sum = dot_first(attn_all, plan.tie(grad_projected, grad_attn_own)).astype(bf16)
    if paired:
        grad_proj = (grad_proj + grad_proj_sent.astype(f32)).astype(bf16)
    first_sum = jnp.concatenate([first_sum, grad_proj, bias_sums.reshape(width, extra)], axis=1)
    stages = []
    first_sum = plan.scatter_last(first_sum, stages)
    if paired:
        grad_attn_own = plan.tie(grad_attn_own, stages[1])
    grad_attn_in = plan.total(grad_attn_own, grad_attn_sent)
    grad_tokens = (
        grad_resid + norm_back(grad_attn_in * (1.0 + scale_one), normed_one, inverse_one)
    ).astype(bf16)
    if not paired:
        branch_two_parts = (plan.total(*branch_two_parts), jnp.zeros(tokens.shape, bf16))
    block_out, gate_two_sum = finish(
        residual_mid, *branch_two_parts, fc2_bias.reshape(1, width), gate_two, grad_out
    )
    sums = [
        jnp.sum(v, axis=0)
        for v in (
            grad_attn_in,
            grad_attn_in * normed_one,
            grad_resid * branch_one,
            grad_mlp_in,
            grad_mlp_in * normed_two,
        )
    ]
    sums = jnp.stack(sums + [gate_two_sum[0]])
    if paired:
        sums = plan.tie(sums, stages[2])
    grad_mod = plan.scatter_columns(sums).astype(bf16)
    if paired:
        grad_mod = plan.tie(grad_mod, stages[3], second_sum)
    grad_mod = plan.gather_dp(grad_mod)
    grad_silu = jnp.einsum("lke,dke->ld", grad_mod, ada_w, preferred_element_type=f32)
    grad_silu = plan.gather_dp(plan.sum_tensor(grad_silu))
    grad_ada_w = jnp.einsum("ld,lke->dke", silu_own, grad_mod, preferred_element_type=f32)
    grad_ada_b = jnp.sum(grad_mod, axis=0, dtype=f32).reshape(6, heads_part, head_size)
    grad_ada_b = lax.dynamic_slice_in_dim(grad_ada_b, dp_index * piece, piece, axis=2)
    grad_silu = lax.dynamic_index_in_dim(grad_silu, dp_index, 1, keepdims=False).reshape(1, width)
    grad_cond = jax.vjp(jax.nn.silu, cond.astype(f32))[1](grad_silu)[0].astype(bf16)

    owned = first_sum[:, qkv_width + part_width :].reshape(-1)[:bias_count].astype(f32)
    grad_qv_b = owned[: qv_b.size].reshape(qv_b.shape)
    start = qv_b.size
    grad_fc1_b = owned[start : start + fc1_b.size].reshape(fc1_b.shape)
    start += fc1_b.size
    return (
        block_out,
        grad_tokens,
        grad_cond,
        grad_ada_w,
        grad_ada_b,
        first_sum[:, :qkv_width].astype(f32).reshape(qkv_w.shape),
        grad_qv_b,
        first_sum[:, qkv_width : qkv_width + part_width].astype(f32).T,
        owned[start : start + shard],
        second_sum[0].astype(f32),
        grad_fc1_b,
        second_sum[1].astype(f32).T,
        owned[start + shard :],
    )


def solution(mesh):
    rows = P(("dp", "tensor"), None)
    ada = P("dp", None, "tensor")
    heads = P(None, "tensor", "dp")
    out = P("tensor", "dp")
    weights = (ada, heads, ada, heads, out, P("dp"), P("dp", "tensor"), out, out, P("dp"))
    return jax.shard_map(
        functools.partial(body, mesh.shape["dp"], mesh.shape["tensor"]),
        mesh=mesh,
        in_specs=(rows, P("dp", None)) + weights + (rows,),
        out_specs=(rows, rows, P("dp", None)) + weights,
        check_vma=False,
    )
```

```python
import functools

import jax
import jax.numpy as jnp
from jax import lax
from jax.experimental import pallas as pl
from jax.experimental.pallas import tpu as pltpu
from jax.sharding import PartitionSpec as P

eps_norm = 1e-06
log2_e = 1.4426950408889634
both_axes = ("dp", "tensor")
f32 = jnp.float32
bf16 = jnp.bfloat16


def normalize(values):
    centre = values - jnp.mean(values, axis=-1, keepdims=True)
    inverse = lax.rsqrt(jnp.mean(centre * centre, axis=-1, keepdims=True) + eps_norm)
    return (centre * inverse, inverse)


def norm_back(grad_normed, normed, inverse):
    first = jnp.mean(grad_normed, axis=-1, keepdims=True)
    second = jnp.mean(grad_normed * normed, axis=-1, keepdims=True)
    return inverse * (grad_normed - first - normed * second)


def gelu_tanh(values):
    return jax.nn.gelu(values, approximate=True)


def dot_rows(left, right):
    return lax.dot_general(left, right, (((1,), (0,)), ((), ())), preferred_element_type=f32)


def dot_last(left, right):
    return lax.dot_general(left, right, (((1,), (1,)), ((), ())), preferred_element_type=f32)


def dot_first(left, right):
    return lax.dot_general(left, right, (((0,), (0,)), ((), ())), preferred_element_type=f32)


def head_masks(lanes, head_size):
    lane = lax.broadcasted_iota(jnp.int32, (1, lanes), 1)
    return [
        (lane >= h * head_size) & (lane < (h + 1) * head_size) for h in range(lanes // head_size)
    ]


def attend_kernel(head_size, q_ref, k_ref, v_ref, out_ref):
    lanes = q_ref.shape[1]
    masks = head_masks(lanes, head_size)
    factor = head_size**-0.5 * log2_e
    queries = q_ref[...]
    keys = k_ref[...]
    values = v_ref[...]
    result = None
    for mask in masks:
        scores = dot_last(jnp.where(mask, queries, jnp.zeros_like(queries)), keys)
        top = jnp.max(scores, axis=1, keepdims=True)
        powers = jnp.exp2((scores - top) * factor)
        total = jnp.sum(powers, axis=1, keepdims=True)
        part = dot_rows(powers.astype(bf16), values) * (1.0 / total)
        result = part if result is None else jnp.where(mask, part, result)
    out_ref[...] = result.astype(bf16)


def attend_back_kernel(head_size, q_ref, k_ref, v_ref, g_ref, *refs):
    out_ref, sum_k, sum_v = refs[-3:]
    lanes = q_ref.shape[1]
    masks = head_masks(lanes, head_size)
    scale = head_size**-0.5
    factor = scale * log2_e
    step = pl.program_id(1)

    @pl.when(step == 0)
    def _():
        queries = q_ref[...]
        grads = g_ref[...]
        keys = k_ref[...]
        values = v_ref[...]
        zero = jnp.zeros_like(keys)
        result = None
        for h, mask in enumerate(masks):
            scores = dot_last(jnp.where(mask, keys, zero), queries)
            top = jnp.max(scores, axis=0, keepdims=True)
            powers = jnp.exp2((scores - top) * factor)
            probs = powers * (1.0 / jnp.sum(powers, axis=0, keepdims=True))
            grad_probs = dot_last(jnp.where(mask, values, zero), grads)
            inner = jnp.sum(probs * grad_probs, axis=0, keepdims=True)
            grad_scores = (probs * (grad_probs - inner)).astype(bf16)
            sum_v[h] = dot_rows(probs.astype(bf16), grads)
            sum_k[h] = dot_rows(grad_scores, queries)
            part = dot_first(grad_scores, keys)
            result = part if result is None else jnp.where(mask, part, result)
        out_ref[...] = (result * scale).astype(bf16)

    def joined(sums):
        total = sums[0]
        for h in range(1, len(masks)):
            total = jnp.where(masks[h], sums[h], total)
        return total

    @pl.when(step == 1)
    def _():
        out_ref[...] = (joined(sum_k) * scale).astype(bf16)

    @pl.when(step == 2)
    def _():
        out_ref[...] = joined(sum_v).astype(bf16)


def column_spec(rows, lanes, first, row_block=0):
    return pl.BlockSpec((rows, lanes), lambda j: (row_block, first + j))


def attention(projected, row_block, row_blocks, part_width, head_size):
    rows = projected.shape[0]
    here = rows // row_blocks
    lanes = min(128, part_width)
    count = part_width // lanes
    work = rows * here * part_width
    return pl.pallas_call(
        functools.partial(attend_kernel, head_size),
        out_shape=jax.ShapeDtypeStruct((here, part_width), bf16),
        grid=(count,),
        in_specs=[
            column_spec(here, lanes, 0, row_block),
            column_spec(rows, lanes, count),
            column_spec(rows, lanes, 2 * count),
        ],
        out_specs=column_spec(here, lanes, 0),
        compiler_params=pltpu.CompilerParams(vmem_limit_bytes=40 * 1024 * 1024),
        cost_estimate=pl.CostEstimate(
            flops=16 * work,
            bytes_accessed=8 * rows * part_width,
            transcendentals=work // head_size,
        ),
    )(projected, projected, projected)


def attention_back(projected, grads, earlier, first, blocks, part_width, head_size):
    rows = projected.shape[0]
    lanes = min(128, part_width)
    count = part_width // lanes
    work = rows * rows * blocks * lanes
    sums = pltpu.VMEM((lanes // head_size, rows, lanes), f32)

    def items(part):
        return pl.BlockSpec((rows, lanes), lambda j, p: (0, part * count + first + j))

    in_specs = [items(0), items(1), items(2), items(0)]
    operands = [projected, projected, projected, grads]
    aliases = {}
    if earlier is not None:
        in_specs.append(pl.BlockSpec(memory_space=pl.ANY))
        operands.append(earlier)
        aliases = {4: 0}
    return pl.pallas_call(
        functools.partial(attend_back_kernel, head_size),
        out_shape=jax.ShapeDtypeStruct((rows, 3 * part_width), bf16),
        grid=(blocks, 3),
        in_specs=in_specs,
        out_specs=pl.BlockSpec((rows, lanes), lambda j, p: (0, p * count + first + j)),
        scratch_shapes=[sums, sums],
        input_output_aliases=aliases,
        compiler_params=pltpu.CompilerParams(vmem_limit_bytes=48 * 1024 * 1024),
        cost_estimate=pl.CostEstimate(
            flops=40 * work,
            bytes_accessed=14 * rows * blocks * lanes,
            transcendentals=work // head_size,
        ),
    )(*operands)


def add_sums(sum_ref, terms):
    @pl.when(pl.program_id(0) == 0)
    def _():
        sum_ref[...] = jnp.zeros_like(sum_ref)

    for number, term in enumerate(terms):
        sum_ref[number : number + 1, :] += jnp.sum(term, axis=0, keepdims=True)


def middle_kernel(tokens_ref, branch_ref, bias_ref, mod_ref, resid_ref, low_ref):
    resid = tokens_ref[...].astype(f32) + mod_ref[2:3, :] * (branch_ref[...] + bias_ref[...])
    resid_ref[...] = resid
    normed, _ = normalize(resid)
    low_ref[...] = (normed * (1.0 + mod_ref[4:5, :]) + mod_ref[3:4, :]).astype(bf16)


def middle_back_kernel(
    resid_ref, branch_ref, own_ref, other_ref, top_ref, bias_ref, mod_ref, grad_ref, low_ref, sum_ref
):
    grad_in = own_ref[...] + other_ref[...].astype(f32)
    normed, inverse = normalize(resid_ref[...])
    back = norm_back(grad_in * (1.0 + mod_ref[4:5, :]), normed, inverse)
    grads = top_ref[...].astype(f32) + back
    grad_ref[...] = grads
    low = (mod_ref[2:3, :] * grads).astype(bf16)
    low_ref[...] = low
    branch = branch_ref[...] + bias_ref[...]
    add_sums(sum_ref, (grads * branch, grad_in, grad_in * normed, low.astype(f32)))


def first_back_kernel(tokens_ref, own_ref, other_ref, grad_ref, mod_ref, out_ref, sum_ref):
    grad_in = own_ref[...] + other_ref[...].astype(f32)
    normed, inverse = normalize(tokens_ref[...].astype(f32))
    back = norm_back(grad_in * (1.0 + mod_ref[1:2, :]), normed, inverse)
    out_ref[...] = (grad_ref[...] + back).astype(bf16)
    add_sums(sum_ref, (grad_in, grad_in * normed))


def finish_kernel(resid_ref, own_ref, other_ref, top_ref, bias_ref, mod_ref, out_ref, sum_ref):
    branch = own_ref[...] + other_ref[...].astype(f32) + bias_ref[...]
    out_ref[...] = (resid_ref[...] + mod_ref[5:6, :] * branch).astype(bf16)
    add_sums(sum_ref, (top_ref[...].astype(f32) * branch,))


def over_rows(kernel, many, single, kinds, summed):
    rows, width = many[0].shape
    block = min(128, rows)
    spec = pl.BlockSpec((block, width), lambda i: (i, 0))
    in_specs = [spec] * len(many)
    in_specs += [pl.BlockSpec(v.shape, lambda i: (0, 0)) for v in single]
    out_specs = [spec] * len(kinds)
    out_shape = [jax.ShapeDtypeStruct((rows, width), kind) for kind in kinds]
    if summed:
        out_specs.append(pl.BlockSpec((8, width), lambda i: (0, 0)))
        out_shape.append(jax.ShapeDtypeStruct((8, width), f32))
    return pl.pallas_call(
        kernel,
        out_shape=out_shape,
        grid=(rows // block,),
        in_specs=in_specs,
        out_specs=out_specs,
        compiler_params=pltpu.CompilerParams(vmem_limit_bytes=32 * 1024 * 1024),
        cost_estimate=pl.CostEstimate(
            flops=20 * rows * width, bytes_accessed=16 * rows * width, transcendentals=0
        ),
    )(*many, *single)


class PairPlan:
    def __init__(self, dp_size):
        self.dp_size = dp_size
        self.index = lax.axis_index("dp")
        self.masks = [1 << b for b in range(dp_size.bit_length() - 1)]
        self.blocks = 2

    def tie(self, values, *others):
        return lax.optimization_barrier((values,) + others)[0]

    def across(self, values):
        return lax.ppermute(values, "tensor", [(0, 1), (1, 0)])

    def swap(self, values, mask):
        return lax.ppermute(values, "dp", [(i, i ^ mask) for i in range(self.dp_size)])

    def upper(self, mask):
        return (self.index // mask) % 2 == 1

    def join(self, own, other, upper, axis):
        return jnp.stack([jnp.where(upper, other, own), jnp.where(upper, own, other)], axis=axis)

    def gather_dp(self, values):
        gathered = values
        for low in self.masks[::2]:
            items = [gathered] + [self.swap(gathered, low * other) for other in (1, 2, 3)]
            place = (self.index // low) % 4
            gathered = jnp.stack([self.choose(items, place ^ slot) for slot in range(4)])
        return gathered.reshape((-1,) + values.shape)

    def choose(self, items, which):
        chosen = items[3]
        for number in range(3):
            chosen = jnp.where(which == number, items[number], chosen)
        return chosen

    def reduce_small(self, values):
        shape = values.shape[1:]
        for low in self.masks[::2][::-1]:
            values = values.reshape((4, -1) + shape)
            place = (self.index // low) % 4
            items = [values[slot] for slot in range(4)]
            total = self.choose(items, place)
            for other in (1, 2, 3):
                total = total + self.swap(self.choose(items, place ^ other), low * other)
            values = total
        return values[0]

    def step(self, values, mask, axis):
        upper = self.upper(mask)
        low = lax.index_in_dim(values, 0, axis, keepdims=False)
        high = lax.index_in_dim(values, 1, axis, keepdims=False)
        return jnp.where(upper, high, low), self.swap(jnp.where(upper, low, high), mask)

    def add(self, own, received):
        return (own.astype(f32) + received.astype(f32)).astype(bf16)

    def hold(self, *values):
        return lax.optimization_barrier(values)

    def send(self, rows):
        return self.across(rows)

    def gather(self, rows, received):
        return [rows, received]

    def scatter(self, term):
        sent = term(1, None).astype(bf16)
        received = self.across(sent)
        return term(0, sent), received

    def pair(self, own, received):
        return own, received

    def columns(self, values):
        other = self.across(values)
        second = lax.axis_index("tensor") == 1
        return jnp.concatenate(
            [jnp.where(second, other, values), jnp.where(second, values, other)], axis=1
        )

    def scatter_columns(self, values):
        half = values.shape[1] // 2
        second = lax.axis_index("tensor") == 1
        low = values[:, :half]
        high = values[:, half:]
        return jnp.where(second, high, low) + self.across(jnp.where(second, low, high))

    def sum_tensor(self, values):
        return values + self.across(values)


class AxisPlan:
    def __init__(self):
        self.blocks = 1

    def tie(self, values, *others):
        return values

    def gather_dp(self, values):
        return lax.all_gather(values, "dp", axis=0)

    def reduce_small(self, values):
        return lax.psum_scatter(values, "dp", scatter_dimension=0, tiled=False)

    def hold(self, *values):
        return values

    def scatter_last(self, grads):
        return lax.psum_scatter(grads, "dp", scatter_dimension=0, tiled=True)

    def send(self, rows):
        return rows

    def gather(self, rows, received):
        return [lax.all_gather(rows, "tensor", axis=0, tiled=True)]

    def scatter(self, term):
        return (
            lax.psum_scatter(term(0, None).astype(bf16), "tensor", scatter_dimension=0, tiled=True),
            None,
        )

    def pair(self, own, received):
        return own.astype(f32), jnp.zeros(own.shape, bf16)

    def columns(self, values):
        return lax.all_gather(values, "tensor", axis=1, tiled=True)

    def scatter_columns(self, values):
        return lax.psum_scatter(values, "tensor", scatter_dimension=1, tiled=True)

    def sum_tensor(self, values):
        return lax.psum(values, "tensor")


def stack_rows(blocks):
    return blocks[0] if len(blocks) == 1 else jnp.concatenate(blocks, axis=0)


def body(
    dp_size,
    parts,
    tokens,
    cond,
    ada_w,
    ada_b,
    qkv_w,
    qv_b,
    proj_w,
    proj_b,
    fc1_w,
    fc1_b,
    fc2_w,
    fc2_b,
    grad_out,
):
    paired = parts == 2 and dp_size in (4, 16, 64)
    plan = PairPlan(dp_size) if paired else AxisPlan()
    dp_index = lax.axis_index("dp")
    width = tokens.shape[1]
    shard = ada_w.shape[0]
    part_width = qkv_w.shape[2]
    hidden_part = fc1_w.shape[1]
    heads_part = qv_b.shape[1]
    piece = qv_b.shape[2]
    head_size = piece * dp_size
    qkv_width = 3 * part_width
    extra = 128
    assert cond.shape[0] == 1

    proj_shard = proj_w.T
    if paired:
        proj_shard = jnp.concatenate([proj_shard, plan.send(proj_shard)], axis=1)
    first_shard = jnp.concatenate([qkv_w.reshape(shard, qkv_width), proj_shard], axis=1)

    def gather_weight(values):
        return lax.all_gather(values, "dp", axis=0, tiled=True)

    def scatter_weight(values):
        return lax.psum_scatter(values, "dp", scatter_dimension=1, tiled=True)

    first_full = gather_weight(first_shard)
    tokens_all = plan.gather(tokens, plan.send(tokens))
    grad_out_sent = plan.send(plan.tie(grad_out, tokens_all[-1]))

    small = plan.gather_dp(
        jnp.concatenate([v.reshape(-1) for v in (cond, proj_b, fc2_b, ada_b, qv_b, fc1_b)])
    )
    mlp_shard = jnp.stack([fc1_w, fc2_w.T])
    mlp_full = lax.all_gather(plan.tie(mlp_shard, small), "dp", axis=1, tiled=True)
    fc1_full = mlp_full[0]
    fc2_full = mlp_full[1]
    start = width + 2 * shard
    cond_all = small[:, :width].astype(f32)
    proj_bias = small[:, width : width + shard].reshape(width).astype(f32)
    fc2_bias = small[:, width + shard : start].reshape(width).astype(f32)
    head_bias = small[:, start:].reshape(dp_size, -1, piece).transpose(1, 0, 2).reshape(-1)
    head_bias = plan.hold(head_bias)[0].astype(f32)
    ada_bias = head_bias[: 6 * part_width].reshape(6, part_width)
    qv_bias = head_bias[6 * part_width : 8 * part_width].reshape(2, part_width)
    fc1_bias = head_bias[8 * part_width :]
    silu_all = jax.nn.silu(cond_all).astype(bf16)
    silu_own = lax.dynamic_slice_in_dim(silu_all, dp_index * shard, shard, axis=1)
    mod_terms = jnp.einsum("ld,dke->lke", silu_own, ada_w, preferred_element_type=f32)
    mod_part = plan.tie(plan.reduce_small(mod_terms) + ada_bias, tokens_all[-1])
    modulation = plan.columns(mod_part)
    shift_one, scale_one, gate_two = [modulation[k : k + 1] for k in (0, 1, 5)]

    attn_blocks = []
    for rows in tokens_all:
        normed, _ = normalize(rows.astype(f32))
        attn_blocks.append((normed * (1.0 + scale_one) + shift_one).astype(bf16))
    qkv_full = first_full[:, :qkv_width]
    qkv_bias = jnp.concatenate([qv_bias[0], jnp.zeros((part_width,), f32), qv_bias[1]])
    attn_all = stack_rows(attn_blocks)
    projected = (dot_rows(attn_all, qkv_full) + qkv_bias).astype(bf16)

    proj_full = first_full[:, qkv_width : qkv_width + part_width]
    far_proj = first_full[:, qkv_width + part_width :]
    grad_two = [
        (gate_two * rows.astype(f32)).astype(bf16) for rows in plan.gather(grad_out, grad_out_sent)
    ]
    grad_two_all = stack_rows(grad_two)
    attended = [None] * plan.blocks

    def rows_of(values, block):
        count = values.shape[0] // plan.blocks
        return values[block * count : (block + 1) * count]

    def attend(block, items):
        return attention(items, block, plan.blocks, part_width, head_size)

    def attend_term(block, earlier):
        attended[block] = attend(block, projected)
        return dot_last(attended[block], proj_full)

    if paired:
        attended_sent = plan.send(attend(1, projected))
        attended_own = attend(0, plan.tie(projected, grad_out_sent))
        branch_one = dot_last(attended_own, proj_full) + dot_last(attended_sent, far_proj)
    else:
        branch_one = plan.scatter(attend_term)[0].astype(f32)
    proj_bias = proj_bias.reshape(1, width)
    fc2_bias = fc2_bias.reshape(1, width)
    residual_mid, mlp_low = over_rows(
        middle_kernel, (tokens, branch_one), (proj_bias, modulation), (f32, bf16), False
    )
    mlp_blocks = plan.gather(mlp_low, plan.send(mlp_low))
    mlp_all = stack_rows(mlp_blocks)
    hidden = [dot_rows(rows, fc1_full) + fc1_bias for rows in mlp_blocks]
    active_blocks = [gelu_tanh(rows).astype(bf16) for rows in hidden]
    active = stack_rows(active_blocks)

    grad_hidden = [None] * plan.blocks

    def mlp_back_term(block, earlier):
        grads = grad_two[block] if earlier is None else plan.tie(grad_two[block], earlier)
        pull = jax.vjp(gelu_tanh, hidden[block])[1]
        grad_hidden[block] = pull(dot_rows(grads, fc2_full))[0].astype(bf16)
        return dot_last(grad_hidden[block], fc1_full)

    grad_mlp_own, grad_mlp_sent = plan.scatter(mlp_back_term)
    grad_hidden_all = stack_rows(grad_hidden)
    mlp_sums = lax.dot_general(
        jnp.stack([mlp_all, grad_two_all]),
        jnp.stack([grad_hidden_all, active]),
        (((1,), (1,)), ((0,), (0,))),
        preferred_element_type=f32,
    ).astype(bf16)
    second_sum = lax.psum_scatter(mlp_sums, "dp", scatter_dimension=1, tiled=True)
    grad_mlp_own = plan.tie(grad_mlp_own, mlp_sums)
    grad_resid, grad_branch_one, middle_sums = over_rows(
        middle_back_kernel,
        (residual_mid, branch_one, *plan.pair(grad_mlp_own, grad_mlp_sent), grad_out),
        (proj_bias, modulation),
        (f32, bf16),
        True,
    )
    proj_sum = middle_sums[3]
    grad_proj_sent = None
    if paired:
        far_grads = dot_rows(grad_branch_one, far_proj).astype(bf16)
        grad_attended_sent = plan.send(far_grads)
        grad_attended = dot_rows(grad_branch_one, proj_full).astype(bf16)
        grad_rows = plan.tie(grad_branch_one, far_grads)
        far_proj_sum = dot_first(grad_rows, attended_sent).astype(bf16)
        grad_proj = dot_first(grad_rows, attended_own).astype(bf16)
        grad_attended_sent = plan.tie(grad_attended_sent, far_proj_sum, grad_proj)
        grad_proj_sent = plan.send(plan.tie(far_proj_sum, grad_attended_sent))
        proj_sum = plan.sum_tensor(plan.tie(proj_sum, grad_attended_sent))
        grad_attended = stack_rows([grad_attended, grad_attended_sent])
    else:
        grad_one_all = stack_rows(plan.gather(grad_branch_one, plan.send(grad_branch_one)))
        proj_sum = jnp.sum(grad_one_all, axis=0, dtype=f32)
        grad_proj = dot_first(grad_one_all, stack_rows(attended)).astype(bf16)
        grad_attended = dot_rows(grad_one_all, proj_full).astype(bf16)

    if paired:
        far_rows = dot_last(plan.tie(active_blocks[1], far_grads), fc2_full).astype(bf16)
    else:
        branch_two = plan.scatter(lambda block, e: dot_last(active_blocks[0], fc2_full))[0]
        branch_two_parts = plan.pair(branch_two, None)

    def token_sum(values):
        return jnp.sum(values, axis=0, dtype=f32)

    head_sums = token_sum(grad_hidden_all)
    head_sums = head_sums.reshape(-1, dp_size, piece).transpose(1, 0, 2).reshape(dp_size, -1)
    bias_sums = jnp.concatenate(
        [
            head_sums,
            proj_sum.reshape(dp_size, shard),
            token_sum(grad_two_all).reshape(dp_size, shard),
        ],
        axis=1,
    ).astype(bf16)
    bias_sums = jnp.pad(bias_sums, ((0, 0), (0, shard * extra - bias_sums.shape[1])))
    bias_sums = bias_sums.reshape(width, extra)
    lane_blocks = part_width // min(128, part_width)
    calls = 2 if lane_blocks % 2 == 0 else 1
    grad_projected = None
    for call in range(calls):
        if call == 1 and paired:
            grad_attended, grad_proj_sent, bias_sums, grad_projected, far_rows = plan.hold(
                grad_attended, grad_proj_sent, bias_sums, grad_projected, far_rows
            )
            own_active, grad_projected = plan.hold(active_blocks[0], grad_projected)
            own_rows, grad_attended = plan.hold(dot_last(own_active, fc2_full), grad_attended)
            branch_two_parts = (own_rows, plan.send(far_rows))
        grad_projected = attention_back(
            projected,
            grad_attended,
            grad_projected,
            call * (lane_blocks // calls),
            lane_blocks // calls,
            part_width,
            head_size,
        )

    def attn_back_term(block, earlier):
        items = rows_of(grad_projected, block)
        if earlier is not None:
            items = plan.tie(items, earlier)
        return dot_last(items, qkv_full)

    if paired:
        branch_two_sent, grad_projected = plan.hold(branch_two_parts[1], grad_projected)
        branch_two_parts = (branch_two_parts[0], branch_two_sent)
    grad_attn_own, grad_attn_sent = plan.scatter(attn_back_term)
    grad_attn_own, grad_projected = plan.hold(grad_attn_own, grad_projected)
    qkv_sums = token_sum(grad_projected)
    first_sum = dot_first(attn_all, grad_projected).astype(bf16)
    if paired:
        grad_proj = plan.add(grad_proj, grad_proj_sent)
    first_sum = jnp.concatenate([first_sum, grad_proj, bias_sums], axis=1)
    if paired:
        first_sum = first_sum.reshape((2, 2, 2, 2, shard, -1))
        half = first_sum.shape[-1] // 256 * 128
        first_sum, grad_attn_sent = plan.hold(first_sum, grad_attn_sent)
        held, received = plan.step(first_sum, 1, 3)
        first_sum = plan.add(held, received)
        one = plan.step(first_sum[..., :half], 2, 2)
        two = plan.step(first_sum[..., half:], 4, 1)
    else:
        first_sum = plan.scatter_last(first_sum)
    block_out, last_sums = over_rows(
        finish_kernel,
        (residual_mid, *branch_two_parts, grad_out),
        (fc2_bias, modulation),
        (bf16,),
        True,
    )
    grad_tokens, first_sums = over_rows(
        first_back_kernel,
        (tokens, *plan.pair(grad_attn_own, grad_attn_sent), grad_resid),
        (modulation,),
        (bf16,),
        True,
    )
    sums = jnp.concatenate([first_sums[:2], middle_sums[:3], last_sums[:1]], axis=0)
    grad_mod = plan.scatter_columns(sums).astype(bf16)
    grad_mod, second_sum = plan.hold(grad_mod, second_sum)
    qv_sums = jnp.stack([qkv_sums[:part_width], qkv_sums[2 * part_width :]]).astype(bf16)
    grad_mod = plan.gather_dp(jnp.concatenate([grad_mod, qv_sums], axis=0))
    qv_sums = jnp.sum(grad_mod[:, 6:], axis=0, dtype=f32).reshape(2, heads_part, head_size)
    grad_qv_b = lax.dynamic_slice_in_dim(qv_sums, dp_index * piece, piece, axis=2)
    grad_mod = grad_mod[:, :6]
    if paired:
        one_sum, two_sum, grad_mod = plan.hold(plan.add(*one), plan.add(*two), grad_mod)
        one = plan.step(one_sum, 4, 1)
        two = plan.step(two_sum, 8, 0)
    grad_silu = jnp.einsum("lke,dke->ld", grad_mod, ada_w, preferred_element_type=f32)
    grad_silu = plan.sum_tensor(grad_silu)
    if paired:
        one_sum, two_sum, grad_silu = plan.hold(plan.add(*one), plan.add(*two), grad_silu)
        one = plan.step(one_sum, 8, 0)
        two = plan.step(two_sum, 2, 0)
    grad_silu = plan.gather_dp(grad_silu)
    if paired:
        first_sum = jnp.concatenate([plan.add(*one), plan.add(*two)], axis=-1)
    grad_ada_w = jnp.einsum("ld,lke->dke", silu_own, grad_mod, preferred_element_type=f32)
    grad_ada_b = jnp.sum(grad_mod, axis=0, dtype=f32).reshape(6, heads_part, head_size)
    grad_ada_b = lax.dynamic_slice_in_dim(grad_ada_b, dp_index * piece, piece, axis=2)
    grad_silu = lax.dynamic_index_in_dim(grad_silu, dp_index, 1, keepdims=False).reshape(1, width)
    grad_cond = jax.vjp(jax.nn.silu, cond.astype(f32))[1](grad_silu)[0].astype(bf16)

    owned = first_sum[:, qkv_width + part_width :].reshape(-1).astype(f32)
    start = fc1_b.size
    grad_fc1_b = owned[:start].reshape(fc1_b.shape)
    return (
        block_out,
        grad_tokens,
        grad_cond,
        grad_ada_w,
        grad_ada_b,
        first_sum[:, :qkv_width].astype(f32).reshape(qkv_w.shape),
        grad_qv_b,
        first_sum[:, qkv_width : qkv_width + part_width].astype(f32).T,
        owned[start : start + shard],
        second_sum[0].astype(f32),
        grad_fc1_b,
        second_sum[1].astype(f32).T,
        owned[start + shard : start + 2 * shard],
    )


def solution(mesh):
    rows = P(("dp", "tensor"), None)
    ada = P("dp", None, "tensor")
    heads = P(None, "tensor", "dp")
    out = P("tensor", "dp")
    weights = (ada, heads, ada, heads, out, P("dp"), P("dp", "tensor"), out, out, P("dp"))
    return jax.shard_map(
        functools.partial(body, mesh.shape["dp"], mesh.shape["tensor"]),
        mesh=mesh,
        in_specs=(rows, P("dp", None)) + weights + (rows,),
        out_specs=(rows, rows, P("dp", None)) + weights,
        check_vma=False,
    )
```

```python
import functools

import jax
import jax.numpy as jnp
from jax import lax
from jax.experimental import pallas as pl
from jax.experimental.pallas import tpu as pltpu
from jax.sharding import PartitionSpec as P

eps_norm = 1e-06
log2_e = 1.4426950408889634
both_axes = ("dp", "tensor")
f32 = jnp.float32
bf16 = jnp.bfloat16


def normalize(values):
    centre = values - jnp.mean(values, axis=-1, keepdims=True)
    inverse = lax.rsqrt(jnp.mean(centre * centre, axis=-1, keepdims=True) + eps_norm)
    return (centre * inverse, inverse)


def norm_back(grad_normed, normed, inverse):
    first = jnp.mean(grad_normed, axis=-1, keepdims=True)
    second = jnp.mean(grad_normed * normed, axis=-1, keepdims=True)
    return inverse * (grad_normed - first - normed * second)


def gelu_tanh(values):
    return jax.nn.gelu(values, approximate=True)


def dot_rows(left, right):
    return lax.dot_general(left, right, (((1,), (0,)), ((), ())), preferred_element_type=f32)


def dot_last(left, right):
    return lax.dot_general(left, right, (((1,), (1,)), ((), ())), preferred_element_type=f32)


def dot_first(left, right):
    return lax.dot_general(left, right, (((0,), (0,)), ((), ())), preferred_element_type=f32)


def head_masks(lanes, head_size):
    lane = lax.broadcasted_iota(jnp.int32, (1, lanes), 1)
    return [
        (lane >= h * head_size) & (lane < (h + 1) * head_size) for h in range(lanes // head_size)
    ]


def attend_kernel(head_size, q_ref, k_ref, v_ref, out_ref):
    lanes = q_ref.shape[1]
    masks = head_masks(lanes, head_size)
    factor = head_size**-0.5 * log2_e
    queries = q_ref[...]
    keys = k_ref[...]
    values = v_ref[...]
    result = None
    for mask in masks:
        scores = dot_last(jnp.where(mask, queries, jnp.zeros_like(queries)), keys)
        top = jnp.max(scores, axis=1, keepdims=True)
        powers = jnp.exp2((scores - top) * factor)
        total = jnp.sum(powers, axis=1, keepdims=True)
        part = dot_rows(powers.astype(bf16), values) * (1.0 / total)
        result = part if result is None else jnp.where(mask, part, result)
    out_ref[...] = result.astype(bf16)


def attend_back_kernel(head_size, q_ref, k_ref, v_ref, g_ref, *refs):
    out_ref, sum_k, sum_v = refs[-3:]
    lanes = q_ref.shape[1]
    masks = head_masks(lanes, head_size)
    scale = head_size**-0.5
    factor = scale * log2_e
    step = pl.program_id(1)

    @pl.when(step == 0)
    def _():
        queries = q_ref[...]
        grads = g_ref[...]
        keys = k_ref[...]
        values = v_ref[...]
        zero = jnp.zeros_like(keys)
        result = None
        for h, mask in enumerate(masks):
            scores = dot_last(jnp.where(mask, keys, zero), queries)
            top = jnp.max(scores, axis=0, keepdims=True)
            powers = jnp.exp2((scores - top) * factor)
            probs = powers * (1.0 / jnp.sum(powers, axis=0, keepdims=True))
            grad_probs = dot_last(jnp.where(mask, values, zero), grads)
            inner = jnp.sum(probs * grad_probs, axis=0, keepdims=True)
            grad_scores = (probs * (grad_probs - inner)).astype(bf16)
            sum_v[h] = dot_rows(probs.astype(bf16), grads)
            sum_k[h] = dot_rows(grad_scores, queries)
            part = dot_first(grad_scores, keys)
            result = part if result is None else jnp.where(mask, part, result)
        out_ref[...] = (result * scale).astype(bf16)

    def joined(sums):
        total = sums[0]
        for h in range(1, len(masks)):
            total = jnp.where(masks[h], sums[h], total)
        return total

    @pl.when(step == 1)
    def _():
        out_ref[...] = (joined(sum_k) * scale).astype(bf16)

    @pl.when(step == 2)
    def _():
        out_ref[...] = joined(sum_v).astype(bf16)


def column_spec(rows, lanes, first, row_block=0):
    return pl.BlockSpec((rows, lanes), lambda j: (row_block, first + j))


def attention(projected, row_block, row_blocks, part_width, head_size):
    rows = projected.shape[0]
    here = rows // row_blocks
    lanes = min(128, part_width)
    count = part_width // lanes
    work = rows * here * part_width
    return pl.pallas_call(
        functools.partial(attend_kernel, head_size),
        out_shape=jax.ShapeDtypeStruct((here, part_width), bf16),
        grid=(count,),
        in_specs=[
            column_spec(here, lanes, 0, row_block),
            column_spec(rows, lanes, count),
            column_spec(rows, lanes, 2 * count),
        ],
        out_specs=column_spec(here, lanes, 0),
        compiler_params=pltpu.CompilerParams(vmem_limit_bytes=40 * 1024 * 1024),
        cost_estimate=pl.CostEstimate(
            flops=16 * work,
            bytes_accessed=8 * rows * part_width,
            transcendentals=work // head_size,
        ),
    )(projected, projected, projected)


def attention_back(projected, grads, earlier, first, blocks, part_width, head_size):
    rows = projected.shape[0]
    lanes = min(128, part_width)
    count = part_width // lanes
    work = rows * rows * blocks * lanes
    sums = pltpu.VMEM((lanes // head_size, rows, lanes), f32)

    def items(part):
        return pl.BlockSpec((rows, lanes), lambda j, p: (0, part * count + first + j))

    in_specs = [items(0), items(1), items(2), items(0)]
    operands = [projected, projected, projected, grads]
    aliases = {}
    if earlier is not None:
        in_specs.append(pl.BlockSpec(memory_space=pl.ANY))
        operands.append(earlier)
        aliases = {4: 0}
    return pl.pallas_call(
        functools.partial(attend_back_kernel, head_size),
        out_shape=jax.ShapeDtypeStruct((rows, 3 * part_width), bf16),
        grid=(blocks, 3),
        in_specs=in_specs,
        out_specs=pl.BlockSpec((rows, lanes), lambda j, p: (0, p * count + first + j)),
        scratch_shapes=[sums, sums],
        input_output_aliases=aliases,
        compiler_params=pltpu.CompilerParams(vmem_limit_bytes=48 * 1024 * 1024),
        cost_estimate=pl.CostEstimate(
            flops=40 * work,
            bytes_accessed=14 * rows * blocks * lanes,
            transcendentals=work // head_size,
        ),
    )(*operands)


def add_sums(sum_ref, terms):
    @pl.when(pl.program_id(0) == 0)
    def _():
        sum_ref[...] = jnp.zeros_like(sum_ref)

    for number, term in enumerate(terms):
        sum_ref[number : number + 1, :] += jnp.sum(term, axis=0, keepdims=True)


def middle_kernel(tokens_ref, branch_ref, bias_ref, mod_ref, resid_ref, low_ref):
    resid = tokens_ref[...].astype(f32) + mod_ref[2:3, :] * (branch_ref[...] + bias_ref[...])
    resid_ref[...] = resid
    normed, _ = normalize(resid)
    low_ref[...] = (normed * (1.0 + mod_ref[4:5, :]) + mod_ref[3:4, :]).astype(bf16)


def middle_back_kernel(
    resid_ref, branch_ref, own_ref, other_ref, top_ref, bias_ref, mod_ref, grad_ref, low_ref, sum_ref
):
    grad_in = own_ref[...] + other_ref[...].astype(f32)
    normed, inverse = normalize(resid_ref[...])
    back = norm_back(grad_in * (1.0 + mod_ref[4:5, :]), normed, inverse)
    grads = top_ref[...].astype(f32) + back
    grad_ref[...] = grads
    low = (mod_ref[2:3, :] * grads).astype(bf16)
    low_ref[...] = low
    branch = branch_ref[...] + bias_ref[...]
    add_sums(sum_ref, (grads * branch, grad_in, grad_in * normed, low.astype(f32)))


def first_back_kernel(tokens_ref, own_ref, other_ref, grad_ref, mod_ref, out_ref, sum_ref):
    grad_in = own_ref[...] + other_ref[...].astype(f32)
    normed, inverse = normalize(tokens_ref[...].astype(f32))
    back = norm_back(grad_in * (1.0 + mod_ref[1:2, :]), normed, inverse)
    out_ref[...] = (grad_ref[...] + back).astype(bf16)
    add_sums(sum_ref, (grad_in, grad_in * normed))


def finish_kernel(resid_ref, own_ref, other_ref, top_ref, bias_ref, mod_ref, out_ref, sum_ref):
    branch = own_ref[...] + other_ref[...].astype(f32) + bias_ref[...]
    out_ref[...] = (resid_ref[...] + mod_ref[5:6, :] * branch).astype(bf16)
    add_sums(sum_ref, (top_ref[...].astype(f32) * branch,))


def over_rows(kernel, many, single, kinds, summed):
    rows, width = many[0].shape
    block = min(128, rows)
    spec = pl.BlockSpec((block, width), lambda i: (i, 0))
    in_specs = [spec] * len(many)
    in_specs += [pl.BlockSpec(v.shape, lambda i: (0, 0)) for v in single]
    out_specs = [spec] * len(kinds)
    out_shape = [jax.ShapeDtypeStruct((rows, width), kind) for kind in kinds]
    if summed:
        out_specs.append(pl.BlockSpec((8, width), lambda i: (0, 0)))
        out_shape.append(jax.ShapeDtypeStruct((8, width), f32))
    return pl.pallas_call(
        kernel,
        out_shape=out_shape,
        grid=(rows // block,),
        in_specs=in_specs,
        out_specs=out_specs,
        compiler_params=pltpu.CompilerParams(vmem_limit_bytes=32 * 1024 * 1024),
        cost_estimate=pl.CostEstimate(
            flops=20 * rows * width, bytes_accessed=16 * rows * width, transcendentals=0
        ),
    )(*many, *single)


class PairPlan:
    def __init__(self, dp_size):
        self.dp_size = dp_size
        self.index = lax.axis_index("dp")
        self.masks = [1 << b for b in range(dp_size.bit_length() - 1)]
        self.blocks = 2

    def tie(self, values, *others):
        return lax.optimization_barrier((values,) + others)[0]

    def across(self, values):
        return lax.ppermute(values, "tensor", [(0, 1), (1, 0)])

    def swap(self, values, mask):
        return lax.ppermute(values, "dp", [(i, i ^ mask) for i in range(self.dp_size)])

    def upper(self, mask):
        return (self.index // mask) % 2 == 1

    def join(self, own, other, upper, axis):
        return jnp.stack([jnp.where(upper, other, own), jnp.where(upper, own, other)], axis=axis)

    def gather_dp(self, values):
        gathered = values
        for low in self.masks[::2]:
            items = [gathered] + [self.swap(gathered, low * other) for other in (1, 2, 3)]
            place = (self.index // low) % 4
            gathered = jnp.stack([self.choose(items, place ^ slot) for slot in range(4)])
        return gathered.reshape((-1,) + values.shape)

    def choose(self, items, which):
        chosen = items[3]
        for number in range(3):
            chosen = jnp.where(which == number, items[number], chosen)
        return chosen

    def reduce_small(self, values):
        shape = values.shape[1:]
        for low in self.masks[::2][::-1]:
            values = values.reshape((4, -1) + shape)
            place = (self.index // low) % 4
            items = [values[slot] for slot in range(4)]
            total = self.choose(items, place)
            for other in (1, 2, 3):
                total = total + self.swap(self.choose(items, place ^ other), low * other)
            values = total
        return values[0]

    def step(self, values, mask, axis):
        upper = self.upper(mask)
        low = lax.index_in_dim(values, 0, axis, keepdims=False)
        high = lax.index_in_dim(values, 1, axis, keepdims=False)
        return jnp.where(upper, high, low), self.swap(jnp.where(upper, low, high), mask)

    def add(self, own, received):
        return (own.astype(f32) + received.astype(f32)).astype(bf16)

    def hold(self, *values):
        return lax.optimization_barrier(values)

    def send(self, rows):
        return self.across(rows)

    def gather(self, rows, received):
        return [rows, received]

    def scatter(self, term):
        sent = term(1, None).astype(bf16)
        received = self.across(sent)
        return term(0, sent), received

    def pair(self, own, received):
        return own, received

    def columns(self, values):
        other = self.across(values)
        second = lax.axis_index("tensor") == 1
        return jnp.concatenate(
            [jnp.where(second, other, values), jnp.where(second, values, other)], axis=1
        )

    def scatter_columns(self, values):
        half = values.shape[1] // 2
        second = lax.axis_index("tensor") == 1
        low = values[:, :half]
        high = values[:, half:]
        return jnp.where(second, high, low) + self.across(jnp.where(second, low, high))

    def sum_tensor(self, values):
        return values + self.across(values)


class AxisPlan:
    def __init__(self):
        self.blocks = 1

    def tie(self, values, *others):
        return values

    def gather_dp(self, values):
        return lax.all_gather(values, "dp", axis=0)

    def reduce_small(self, values):
        return lax.psum_scatter(values, "dp", scatter_dimension=0, tiled=False)

    def hold(self, *values):
        return values

    def scatter_last(self, grads):
        return lax.psum_scatter(grads, "dp", scatter_dimension=0, tiled=True)

    def send(self, rows):
        return rows

    def gather(self, rows, received):
        return [lax.all_gather(rows, "tensor", axis=0, tiled=True)]

    def scatter(self, term):
        return (
            lax.psum_scatter(term(0, None).astype(bf16), "tensor", scatter_dimension=0, tiled=True),
            None,
        )

    def pair(self, own, received):
        return own.astype(f32), jnp.zeros(own.shape, bf16)

    def columns(self, values):
        return lax.all_gather(values, "tensor", axis=1, tiled=True)

    def scatter_columns(self, values):
        return lax.psum_scatter(values, "tensor", scatter_dimension=1, tiled=True)

    def sum_tensor(self, values):
        return lax.psum(values, "tensor")


def stack_rows(blocks):
    return blocks[0] if len(blocks) == 1 else jnp.concatenate(blocks, axis=0)


def body(
    dp_size,
    parts,
    tokens,
    cond,
    ada_w,
    ada_b,
    qkv_w,
    qv_b,
    proj_w,
    proj_b,
    fc1_w,
    fc1_b,
    fc2_w,
    fc2_b,
    grad_out,
):
    paired = parts == 2 and dp_size in (4, 16, 64)
    plan = PairPlan(dp_size) if paired else AxisPlan()
    dp_index = lax.axis_index("dp")
    width = tokens.shape[1]
    shard = ada_w.shape[0]
    part_width = qkv_w.shape[2]
    hidden_part = fc1_w.shape[1]
    heads_part = qv_b.shape[1]
    piece = qv_b.shape[2]
    head_size = piece * dp_size
    qkv_width = 3 * part_width
    extra = 128
    assert cond.shape[0] == 1

    proj_shard = proj_w.T
    if paired:
        proj_shard = jnp.concatenate([proj_shard, plan.send(proj_shard)], axis=1)
    first_shard = jnp.concatenate([qkv_w.reshape(shard, qkv_width), proj_shard], axis=1)

    def gather_weight(values):
        return lax.all_gather(values, "dp", axis=0, tiled=True)

    def scatter_weight(values):
        return lax.psum_scatter(values, "dp", scatter_dimension=1, tiled=True)

    first_full = gather_weight(first_shard)
    tokens_all = plan.gather(tokens, plan.send(tokens))
    grad_out_sent = plan.send(plan.tie(grad_out, tokens_all[-1]))

    small = plan.gather_dp(
        jnp.concatenate([v.reshape(-1) for v in (cond, proj_b, fc2_b, ada_b, qv_b, fc1_b)])
    )
    mlp_shard = jnp.stack([fc1_w, fc2_w.T])
    mlp_full = lax.all_gather(plan.tie(mlp_shard, small), "dp", axis=1, tiled=True)
    fc1_full = mlp_full[0]
    fc2_full = mlp_full[1]
    start = width + 2 * shard
    cond_all = small[:, :width].astype(f32)
    proj_bias = small[:, width : width + shard].reshape(width).astype(f32)
    fc2_bias = small[:, width + shard : start].reshape(width).astype(f32)
    head_bias = small[:, start:].reshape(dp_size, -1, piece).transpose(1, 0, 2).reshape(-1)
    head_bias = plan.hold(head_bias)[0].astype(f32)
    ada_bias = head_bias[: 6 * part_width].reshape(6, part_width)
    qv_bias = head_bias[6 * part_width : 8 * part_width].reshape(2, part_width)
    fc1_bias = head_bias[8 * part_width :]
    silu_all = jax.nn.silu(cond_all).astype(bf16)
    silu_own = lax.dynamic_slice_in_dim(silu_all, dp_index * shard, shard, axis=1)
    mod_terms = jnp.einsum("ld,dke->lke", silu_own, ada_w, preferred_element_type=f32)
    mod_part = plan.tie(plan.reduce_small(mod_terms) + ada_bias, tokens_all[-1])
    modulation = plan.columns(mod_part)
    shift_one, scale_one, gate_two = [modulation[k : k + 1] for k in (0, 1, 5)]

    attn_blocks = []
    for rows in tokens_all:
        normed, _ = normalize(rows.astype(f32))
        attn_blocks.append((normed * (1.0 + scale_one) + shift_one).astype(bf16))
    qkv_full = first_full[:, :qkv_width]
    qkv_bias = jnp.concatenate([qv_bias[0], jnp.zeros((part_width,), f32), qv_bias[1]])
    attn_all = stack_rows(attn_blocks)
    projected = (dot_rows(attn_all, qkv_full) + qkv_bias).astype(bf16)

    proj_full = first_full[:, qkv_width : qkv_width + part_width]
    far_proj = first_full[:, qkv_width + part_width :]
    grad_two = [
        (gate_two * rows.astype(f32)).astype(bf16) for rows in plan.gather(grad_out, grad_out_sent)
    ]
    grad_two_all = stack_rows(grad_two)
    attended = [None] * plan.blocks

    def rows_of(values, block):
        count = values.shape[0] // plan.blocks
        return values[block * count : (block + 1) * count]

    def attend(block, items):
        return attention(items, block, plan.blocks, part_width, head_size)

    def attend_term(block, earlier):
        attended[block] = attend(block, projected)
        return dot_last(attended[block], proj_full)

    if paired:
        attended_sent = plan.send(attend(1, projected))
        attended_own = attend(0, plan.tie(projected, grad_out_sent))
        branch_one = dot_last(attended_own, proj_full) + dot_last(attended_sent, far_proj)
    else:
        branch_one = plan.scatter(attend_term)[0].astype(f32)
    proj_bias = proj_bias.reshape(1, width)
    fc2_bias = fc2_bias.reshape(1, width)
    residual_mid, mlp_low = over_rows(
        middle_kernel, (tokens, branch_one), (proj_bias, modulation), (f32, bf16), False
    )
    mlp_blocks = plan.gather(mlp_low, plan.send(mlp_low))
    mlp_all = stack_rows(mlp_blocks)
    active_blocks = [None] * plan.blocks

    grad_hidden = [None] * plan.blocks

    def mlp_back_term(block, earlier):
        grads, rows = grad_two[block], mlp_blocks[block]
        if earlier is not None:
            grads, rows, _ = plan.hold(grads, rows, earlier)
        hidden = dot_rows(rows, fc1_full) + fc1_bias
        activated, pull = jax.vjp(gelu_tanh, hidden)
        active_blocks[block] = activated.astype(bf16)
        grad_hidden[block] = pull(dot_rows(grads, fc2_full))[0].astype(bf16)
        return dot_last(grad_hidden[block], fc1_full)

    grad_mlp_own, grad_mlp_sent = plan.scatter(mlp_back_term)
    grad_hidden_all = stack_rows(grad_hidden)
    active = stack_rows(active_blocks)
    mlp_sums = lax.dot_general(
        jnp.stack([mlp_all, grad_two_all]),
        jnp.stack([grad_hidden_all, active]),
        (((1,), (1,)), ((0,), (0,))),
        preferred_element_type=f32,
    ).astype(bf16)
    second_sum = lax.psum_scatter(mlp_sums, "dp", scatter_dimension=1, tiled=True)
    grad_mlp_own = plan.tie(grad_mlp_own, mlp_sums)
    grad_resid, grad_branch_one, middle_sums = over_rows(
        middle_back_kernel,
        (residual_mid, branch_one, *plan.pair(grad_mlp_own, grad_mlp_sent), grad_out),
        (proj_bias, modulation),
        (f32, bf16),
        True,
    )
    proj_sum = middle_sums[3]
    grad_proj_sent = None
    if paired:
        far_grads = dot_rows(grad_branch_one, far_proj).astype(bf16)
        grad_attended_sent = plan.send(far_grads)
        grad_attended = dot_rows(grad_branch_one, proj_full).astype(bf16)
        grad_rows = plan.tie(grad_branch_one, far_grads)
        far_proj_sum = dot_first(grad_rows, attended_sent).astype(bf16)
        grad_proj = dot_first(grad_rows, attended_own).astype(bf16)
        grad_attended_sent = plan.tie(grad_attended_sent, far_proj_sum, grad_proj)
        grad_proj_sent = plan.send(plan.tie(far_proj_sum, grad_attended_sent))
        proj_sum = plan.sum_tensor(plan.tie(proj_sum, grad_attended_sent))
        grad_attended = stack_rows([grad_attended, grad_attended_sent])
    else:
        grad_one_all = stack_rows(plan.gather(grad_branch_one, plan.send(grad_branch_one)))
        proj_sum = jnp.sum(grad_one_all, axis=0, dtype=f32)
        grad_proj = dot_first(grad_one_all, stack_rows(attended)).astype(bf16)
        grad_attended = dot_rows(grad_one_all, proj_full).astype(bf16)

    if paired:
        far_rows = dot_last(plan.tie(active_blocks[1], far_grads), fc2_full).astype(bf16)
    else:
        branch_two = plan.scatter(lambda block, e: dot_last(active_blocks[0], fc2_full))[0]
        branch_two_parts = plan.pair(branch_two, None)

    def token_sum(values):
        return jnp.sum(values, axis=0, dtype=f32)

    head_sums = token_sum(grad_hidden_all)
    head_sums = head_sums.reshape(-1, dp_size, piece).transpose(1, 0, 2).reshape(dp_size, -1)
    bias_sums = jnp.concatenate(
        [
            head_sums,
            proj_sum.reshape(dp_size, shard),
            token_sum(grad_two_all).reshape(dp_size, shard),
        ],
        axis=1,
    ).astype(bf16)
    bias_sums = jnp.pad(bias_sums, ((0, 0), (0, shard * extra - bias_sums.shape[1])))
    bias_sums = bias_sums.reshape(width, extra)
    lane_blocks = part_width // min(128, part_width)
    calls = 2 if lane_blocks % 2 == 0 else 1
    grad_projected = None
    for call in range(calls):
        if call == 1 and paired:
            grad_attended, grad_proj_sent, bias_sums, grad_projected, far_rows = plan.hold(
                grad_attended, grad_proj_sent, bias_sums, grad_projected, far_rows
            )
            branch_two_sent = plan.send(far_rows)
        grad_projected = attention_back(
            projected,
            grad_attended,
            grad_projected,
            call * (lane_blocks // calls),
            lane_blocks // calls,
            part_width,
            head_size,
        )

    def attn_back_term(block, earlier):
        items = rows_of(grad_projected, block)
        if earlier is not None:
            items = plan.tie(items, earlier)
        return dot_last(items, qkv_full)

    if paired:
        branch_two_sent, grad_projected = plan.hold(branch_two_sent, grad_projected)
    grad_attn_own, grad_attn_sent = plan.scatter(attn_back_term)
    if paired:
        own_active, grad_attn_own = plan.hold(active_blocks[0], grad_attn_own)
        branch_two_parts = (dot_last(own_active, fc2_full), branch_two_sent)
    block_out, last_sums = over_rows(
        finish_kernel,
        (residual_mid, *branch_two_parts, grad_out),
        (fc2_bias, modulation),
        (bf16,),
        True,
    )
    grad_attn_own, grad_projected, block_out, last_sums = plan.hold(
        grad_attn_own, grad_projected, block_out, last_sums
    )
    qkv_sums = token_sum(grad_projected)
    qv_sums = jnp.stack([qkv_sums[:part_width], qkv_sums[2 * part_width :]]).astype(bf16)
    first_sum = dot_first(attn_all, grad_projected).astype(bf16)
    if paired:
        grad_proj = plan.add(grad_proj, grad_proj_sent)
    first_sum = jnp.concatenate([first_sum, grad_proj, bias_sums], axis=1)
    if paired:
        first_sum = first_sum.reshape((2, 2, 2, 2, shard, -1))
        half = first_sum.shape[-1] // 256 * 128
        first_sum, grad_attn_sent, qv_sums = plan.hold(first_sum, grad_attn_sent, qv_sums)
        held, received = plan.step(first_sum, 1, 3)
        first_sum = plan.add(held, received)
        one = plan.step(first_sum[..., :half], 2, 2)
        two = plan.step(first_sum[..., half:], 4, 1)
    else:
        first_sum = plan.scatter_last(first_sum)
    grad_tokens, first_sums = over_rows(
        first_back_kernel,
        (tokens, *plan.pair(grad_attn_own, grad_attn_sent), grad_resid),
        (modulation,),
        (bf16,),
        True,
    )
    sums = jnp.concatenate([first_sums[:2], middle_sums[:3], last_sums[:1]], axis=0)
    grad_mod = plan.scatter_columns(sums).astype(bf16)
    grad_mod, second_sum = plan.hold(grad_mod, second_sum)
    grad_mod = plan.gather_dp(jnp.concatenate([grad_mod, qv_sums], axis=0))
    qv_sums = jnp.sum(grad_mod[:, 6:], axis=0, dtype=f32).reshape(2, heads_part, head_size)
    grad_qv_b = lax.dynamic_slice_in_dim(qv_sums, dp_index * piece, piece, axis=2)
    grad_mod = grad_mod[:, :6]
    if paired:
        one_sent, two_sent, grad_mod = plan.hold(one[1], two[1], grad_mod)
        one = plan.step(plan.add(one[0], one_sent), 4, 1)
        two = plan.step(plan.add(two[0], two_sent), 8, 0)
    grad_silu = jnp.einsum("lke,dke->ld", grad_mod, ada_w, preferred_element_type=f32)
    grad_silu = plan.sum_tensor(grad_silu)
    if paired:
        one_sent, two_sent, grad_silu = plan.hold(one[1], two[1], grad_silu)
        one = plan.step(plan.add(one[0], one_sent), 8, 0)
        two = plan.step(plan.add(two[0], two_sent), 2, 0)
    grad_silu = plan.gather_dp(grad_silu)
    if paired:
        first_sum = jnp.concatenate([plan.add(*one), plan.add(*two)], axis=-1)
    grad_ada_w = jnp.einsum("ld,lke->dke", silu_own, grad_mod, preferred_element_type=f32)
    grad_ada_b = jnp.sum(grad_mod, axis=0, dtype=f32).reshape(6, heads_part, head_size)
    grad_ada_b = lax.dynamic_slice_in_dim(grad_ada_b, dp_index * piece, piece, axis=2)
    grad_silu = lax.dynamic_index_in_dim(grad_silu, dp_index, 1, keepdims=False).reshape(1, width)
    grad_cond = jax.vjp(jax.nn.silu, cond.astype(f32))[1](grad_silu)[0].astype(bf16)

    owned = first_sum[:, qkv_width + part_width :].reshape(-1).astype(f32)
    start = fc1_b.size
    grad_fc1_b = owned[:start].reshape(fc1_b.shape)
    return (
        block_out,
        grad_tokens,
        grad_cond,
        grad_ada_w,
        grad_ada_b,
        first_sum[:, :qkv_width].astype(f32).reshape(qkv_w.shape),
        grad_qv_b,
        first_sum[:, qkv_width : qkv_width + part_width].astype(f32).T,
        owned[start : start + shard],
        second_sum[0].astype(f32),
        grad_fc1_b,
        second_sum[1].astype(f32).T,
        owned[start + shard : start + 2 * shard],
    )


def solution(mesh):
    rows = P(("dp", "tensor"), None)
    ada = P("dp", None, "tensor")
    heads = P(None, "tensor", "dp")
    out = P("tensor", "dp")
    weights = (ada, heads, ada, heads, out, P("dp"), P("dp", "tensor"), out, out, P("dp"))
    return jax.shard_map(
        functools.partial(body, mesh.shape["dp"], mesh.shape["tensor"]),
        mesh=mesh,
        in_specs=(rows, P("dp", None)) + weights + (rows,),
        out_specs=(rows, rows, P("dp", None)) + weights,
        check_vma=False,
    )
```

```python
import functools

import jax
import jax.numpy as jnp
from jax import lax
from jax.experimental import pallas as pl
from jax.experimental.pallas import tpu as pltpu
from jax.sharding import PartitionSpec as P

eps_norm = 1e-06
log2_e = 1.4426950408889634
both_axes = ("dp", "tensor")
f32 = jnp.float32
bf16 = jnp.bfloat16


def normalize(values):
    centre = values - jnp.mean(values, axis=-1, keepdims=True)
    inverse = lax.rsqrt(jnp.mean(centre * centre, axis=-1, keepdims=True) + eps_norm)
    return (centre * inverse, inverse)


def norm_back(grad_normed, normed, inverse):
    first = jnp.mean(grad_normed, axis=-1, keepdims=True)
    second = jnp.mean(grad_normed * normed, axis=-1, keepdims=True)
    return inverse * (grad_normed - first - normed * second)


def gelu_tanh(values):
    return jax.nn.gelu(values, approximate=True)


def dot_rows(left, right):
    return lax.dot_general(left, right, (((1,), (0,)), ((), ())), preferred_element_type=f32)


def dot_last(left, right):
    return lax.dot_general(left, right, (((1,), (1,)), ((), ())), preferred_element_type=f32)


def dot_first(left, right):
    return lax.dot_general(left, right, (((0,), (0,)), ((), ())), preferred_element_type=f32)


def head_masks(lanes, head_size):
    lane = lax.broadcasted_iota(jnp.int32, (1, lanes), 1)
    return [
        (lane >= h * head_size) & (lane < (h + 1) * head_size) for h in range(lanes // head_size)
    ]


def attend_kernel(head_size, q_ref, k_ref, v_ref, out_ref):
    lanes = q_ref.shape[1]
    masks = head_masks(lanes, head_size)
    factor = head_size**-0.5 * log2_e
    queries = q_ref[...]
    keys = k_ref[...]
    values = v_ref[...]
    result = None
    for mask in masks:
        scores = dot_last(jnp.where(mask, queries, jnp.zeros_like(queries)), keys)
        top = jnp.max(scores, axis=1, keepdims=True)
        powers = jnp.exp2((scores - top) * factor)
        total = jnp.sum(powers, axis=1, keepdims=True)
        part = dot_rows(powers.astype(bf16), values) * (1.0 / total)
        result = part if result is None else jnp.where(mask, part, result)
    out_ref[...] = result.astype(bf16)


def attend_back_kernel(head_size, q_ref, k_ref, v_ref, g_ref, *refs):
    out_ref, sum_k, sum_v = refs[-3:]
    lanes = q_ref.shape[1]
    masks = head_masks(lanes, head_size)
    scale = head_size**-0.5
    factor = scale * log2_e
    step = pl.program_id(1)

    @pl.when(step == 0)
    def _():
        queries = q_ref[...]
        grads = g_ref[...]
        keys = k_ref[...]
        values = v_ref[...]
        zero = jnp.zeros_like(keys)
        result = None
        for h, mask in enumerate(masks):
            scores = dot_last(jnp.where(mask, keys, zero), queries)
            top = jnp.max(scores, axis=0, keepdims=True)
            powers = jnp.exp2((scores - top) * factor)
            probs = powers * (1.0 / jnp.sum(powers, axis=0, keepdims=True))
            grad_probs = dot_last(jnp.where(mask, values, zero), grads)
            inner = jnp.sum(probs * grad_probs, axis=0, keepdims=True)
            grad_scores = (probs * (grad_probs - inner)).astype(bf16)
            sum_v[h] = dot_rows(probs.astype(bf16), grads)
            sum_k[h] = dot_rows(grad_scores, queries)
            part = dot_first(grad_scores, keys)
            result = part if result is None else jnp.where(mask, part, result)
        out_ref[...] = (result * scale).astype(bf16)

    def joined(sums):
        total = sums[0]
        for h in range(1, len(masks)):
            total = jnp.where(masks[h], sums[h], total)
        return total

    @pl.when(step == 1)
    def _():
        out_ref[...] = (joined(sum_k) * scale).astype(bf16)

    @pl.when(step == 2)
    def _():
        out_ref[...] = joined(sum_v).astype(bf16)


def column_spec(rows, lanes, first, row_block=0):
    return pl.BlockSpec((rows, lanes), lambda j: (row_block, first + j))


def attention(projected, row_block, row_blocks, part_width, head_size):
    rows = projected.shape[0]
    here = rows // row_blocks
    lanes = min(128, part_width)
    count = part_width // lanes
    work = rows * here * part_width
    return pl.pallas_call(
        functools.partial(attend_kernel, head_size),
        out_shape=jax.ShapeDtypeStruct((here, part_width), bf16),
        grid=(count,),
        in_specs=[
            column_spec(here, lanes, 0, row_block),
            column_spec(rows, lanes, count),
            column_spec(rows, lanes, 2 * count),
        ],
        out_specs=column_spec(here, lanes, 0),
        compiler_params=pltpu.CompilerParams(vmem_limit_bytes=60 * 1024 * 1024),
        cost_estimate=pl.CostEstimate(
            flops=16 * work,
            bytes_accessed=8 * rows * part_width,
            transcendentals=work // head_size,
        ),
    )(projected, projected, projected)


def attention_back(projected, grads, earlier, first, blocks, part_width, head_size):
    rows = projected.shape[0]
    lanes = min(128, part_width)
    count = part_width // lanes
    work = rows * rows * blocks * lanes
    sums = pltpu.VMEM((lanes // head_size, rows, lanes), f32)

    def items(part):
        return pl.BlockSpec((rows, lanes), lambda j, p: (0, part * count + first + j))

    in_specs = [items(0), items(1), items(2), items(0)]
    operands = [projected, projected, projected, grads]
    aliases = {}
    if earlier is not None:
        in_specs.append(pl.BlockSpec(memory_space=pl.ANY))
        operands.append(earlier)
        aliases = {4: 0}
    return pl.pallas_call(
        functools.partial(attend_back_kernel, head_size),
        out_shape=jax.ShapeDtypeStruct((rows, 3 * part_width), bf16),
        grid=(blocks, 3),
        in_specs=in_specs,
        out_specs=pl.BlockSpec((rows, lanes), lambda j, p: (0, p * count + first + j)),
        scratch_shapes=[sums, sums],
        input_output_aliases=aliases,
        compiler_params=pltpu.CompilerParams(vmem_limit_bytes=60 * 1024 * 1024),
        cost_estimate=pl.CostEstimate(
            flops=40 * work,
            bytes_accessed=14 * rows * blocks * lanes,
            transcendentals=work // head_size,
        ),
    )(*operands)


def add_sums(sum_ref, terms):
    @pl.when(pl.program_id(0) == 0)
    def _():
        sum_ref[...] = jnp.zeros_like(sum_ref)

    for number, term in enumerate(terms):
        sum_ref[number : number + 1, :] += jnp.sum(term, axis=0, keepdims=True)


def middle_kernel(tokens_ref, branch_ref, bias_ref, mod_ref, resid_ref, low_ref):
    resid = tokens_ref[...].astype(f32) + mod_ref[2:3, :] * (branch_ref[...] + bias_ref[...])
    resid_ref[...] = resid
    normed, _ = normalize(resid)
    low_ref[...] = (normed * (1.0 + mod_ref[4:5, :]) + mod_ref[3:4, :]).astype(bf16)


def middle_back_kernel(
    resid_ref, branch_ref, own_ref, other_ref, top_ref, bias_ref, mod_ref, grad_ref, low_ref, sum_ref
):
    grad_in = own_ref[...] + other_ref[...].astype(f32)
    normed, inverse = normalize(resid_ref[...])
    back = norm_back(grad_in * (1.0 + mod_ref[4:5, :]), normed, inverse)
    grads = top_ref[...].astype(f32) + back
    grad_ref[...] = grads
    low = (mod_ref[2:3, :] * grads).astype(bf16)
    low_ref[...] = low
    branch = branch_ref[...] + bias_ref[...]
    add_sums(sum_ref, (grads * branch, grad_in, grad_in * normed, low.astype(f32)))


def first_back_kernel(tokens_ref, own_ref, other_ref, grad_ref, mod_ref, out_ref, sum_ref):
    grad_in = own_ref[...] + other_ref[...].astype(f32)
    normed, inverse = normalize(tokens_ref[...].astype(f32))
    back = norm_back(grad_in * (1.0 + mod_ref[1:2, :]), normed, inverse)
    out_ref[...] = (grad_ref[...] + back).astype(bf16)
    add_sums(sum_ref, (grad_in, grad_in * normed))


def finish_kernel(resid_ref, own_ref, other_ref, top_ref, bias_ref, mod_ref, out_ref, sum_ref):
    branch = own_ref[...] + other_ref[...].astype(f32) + bias_ref[...]
    out_ref[...] = (resid_ref[...] + mod_ref[5:6, :] * branch).astype(bf16)
    add_sums(sum_ref, (top_ref[...].astype(f32) * branch,))


def over_rows(kernel, many, single, kinds, summed):
    rows, width = many[0].shape
    block = min(128, rows)
    spec = pl.BlockSpec((block, width), lambda i: (i, 0))
    in_specs = [spec] * len(many)
    in_specs += [pl.BlockSpec(v.shape, lambda i: (0, 0)) for v in single]
    out_specs = [spec] * len(kinds)
    out_shape = [jax.ShapeDtypeStruct((rows, width), kind) for kind in kinds]
    if summed:
        out_specs.append(pl.BlockSpec((8, width), lambda i: (0, 0)))
        out_shape.append(jax.ShapeDtypeStruct((8, width), f32))
    return pl.pallas_call(
        kernel,
        out_shape=out_shape,
        grid=(rows // block,),
        in_specs=in_specs,
        out_specs=out_specs,
        compiler_params=pltpu.CompilerParams(vmem_limit_bytes=32 * 1024 * 1024),
        cost_estimate=pl.CostEstimate(
            flops=20 * rows * width, bytes_accessed=16 * rows * width, transcendentals=0
        ),
    )(*many, *single)


class PairPlan:
    def __init__(self, dp_size):
        self.dp_size = dp_size
        self.index = lax.axis_index("dp")
        self.masks = [1 << b for b in range(dp_size.bit_length() - 1)]
        self.blocks = 2

    def tie(self, values, *others):
        return lax.optimization_barrier((values,) + others)[0]

    def across(self, values):
        return lax.ppermute(values, "tensor", [(0, 1), (1, 0)])

    def swap(self, values, mask):
        return lax.ppermute(values, "dp", [(i, i ^ mask) for i in range(self.dp_size)])

    def upper(self, mask):
        return (self.index // mask) % 2 == 1

    def join(self, own, other, upper, axis):
        return jnp.stack([jnp.where(upper, other, own), jnp.where(upper, own, other)], axis=axis)

    def gather_dp(self, values):
        gathered = values
        for low in self.masks[::2]:
            items = [gathered] + [self.swap(gathered, low * other) for other in (1, 2, 3)]
            place = (self.index // low) % 4
            gathered = jnp.stack([self.choose(items, place ^ slot) for slot in range(4)])
        return gathered.reshape((-1,) + values.shape)

    def choose(self, items, which):
        chosen = items[3]
        for number in range(3):
            chosen = jnp.where(which == number, items[number], chosen)
        return chosen

    def reduce_small(self, values):
        shape = values.shape[1:]
        for low in self.masks[::2][::-1]:
            values = values.reshape((4, -1) + shape)
            place = (self.index // low) % 4
            items = [values[slot] for slot in range(4)]
            total = self.choose(items, place)
            for other in (1, 2, 3):
                total = total + self.swap(self.choose(items, place ^ other), low * other)
            values = total
        return values[0]

    def step(self, values, mask, axis):
        upper = self.upper(mask)
        low = lax.index_in_dim(values, 0, axis, keepdims=False)
        high = lax.index_in_dim(values, 1, axis, keepdims=False)
        return jnp.where(upper, high, low), self.swap(jnp.where(upper, low, high), mask)

    def add(self, own, received):
        return (own.astype(f32) + received.astype(f32)).astype(bf16)

    def hold(self, *values):
        return lax.optimization_barrier(values)

    def send(self, rows):
        return self.across(rows)

    def gather(self, rows, received):
        return [rows, received]

    def scatter(self, term):
        sent = term(1, None).astype(bf16)
        received = self.across(sent)
        return term(0, sent), received

    def pair(self, own, received):
        return own, received

    def columns(self, values):
        other = self.across(values)
        second = lax.axis_index("tensor") == 1
        return jnp.concatenate(
            [jnp.where(second, other, values), jnp.where(second, values, other)], axis=1
        )

    def scatter_columns(self, values):
        half = values.shape[1] // 2
        second = lax.axis_index("tensor") == 1
        low = values[:, :half]
        high = values[:, half:]
        return jnp.where(second, high, low) + self.across(jnp.where(second, low, high))

    def sum_tensor(self, values):
        return values + self.across(values)


class AxisPlan:
    def __init__(self):
        self.blocks = 1

    def tie(self, values, *others):
        return values

    def gather_dp(self, values):
        return lax.all_gather(values, "dp", axis=0)

    def reduce_small(self, values):
        return lax.psum_scatter(values, "dp", scatter_dimension=0, tiled=False)

    def hold(self, *values):
        return values

    def scatter_last(self, grads):
        return lax.psum_scatter(grads, "dp", scatter_dimension=0, tiled=True)

    def send(self, rows):
        return rows

    def gather(self, rows, received):
        return [lax.all_gather(rows, "tensor", axis=0, tiled=True)]

    def scatter(self, term):
        return (
            lax.psum_scatter(term(0, None).astype(bf16), "tensor", scatter_dimension=0, tiled=True),
            None,
        )

    def pair(self, own, received):
        return own.astype(f32), jnp.zeros(own.shape, bf16)

    def columns(self, values):
        return lax.all_gather(values, "tensor", axis=1, tiled=True)

    def scatter_columns(self, values):
        return lax.psum_scatter(values, "tensor", scatter_dimension=1, tiled=True)

    def sum_tensor(self, values):
        return lax.psum(values, "tensor")


def stack_rows(blocks):
    return blocks[0] if len(blocks) == 1 else jnp.concatenate(blocks, axis=0)


def body(
    dp_size,
    parts,
    tokens,
    cond,
    ada_w,
    ada_b,
    qkv_w,
    qv_b,
    proj_w,
    proj_b,
    fc1_w,
    fc1_b,
    fc2_w,
    fc2_b,
    grad_out,
):
    paired = parts == 2 and dp_size in (4, 16, 64)
    plan = PairPlan(dp_size) if paired else AxisPlan()
    dp_index = lax.axis_index("dp")
    width = tokens.shape[1]
    shard = ada_w.shape[0]
    part_width = qkv_w.shape[2]
    hidden_part = fc1_w.shape[1]
    heads_part = qv_b.shape[1]
    piece = qv_b.shape[2]
    head_size = piece * dp_size
    qkv_width = 3 * part_width
    extra = 128
    assert cond.shape[0] == 1

    proj_shard = proj_w.T
    if paired:
        proj_shard = jnp.concatenate([proj_shard, plan.send(proj_shard)], axis=1)
    first_shard = jnp.concatenate([qkv_w.reshape(shard, qkv_width), proj_shard], axis=1)

    def gather_weight(values):
        return lax.all_gather(values, "dp", axis=0, tiled=True)

    def scatter_weight(values):
        return lax.psum_scatter(values, "dp", scatter_dimension=1, tiled=True)

    first_full = gather_weight(first_shard)
    tokens_all = plan.gather(tokens, plan.send(tokens))
    grad_out_sent = plan.send(plan.tie(grad_out, tokens_all[-1]))

    small = plan.gather_dp(
        jnp.concatenate([v.reshape(-1) for v in (cond, proj_b, fc2_b, ada_b, qv_b, fc1_b)])
    )
    mlp_shard = jnp.stack([fc1_w, fc2_w.T])
    mlp_full = lax.all_gather(plan.tie(mlp_shard, small), "dp", axis=1, tiled=True)
    fc1_full = mlp_full[0]
    fc2_full = mlp_full[1]
    start = width + 2 * shard
    cond_all = small[:, :width].astype(f32)
    proj_bias = small[:, width : width + shard].reshape(width).astype(f32)
    fc2_bias = small[:, width + shard : start].reshape(width).astype(f32)
    head_bias = small[:, start:].reshape(dp_size, -1, piece).transpose(1, 0, 2).reshape(-1)
    head_bias = plan.hold(head_bias)[0].astype(f32)
    ada_bias = head_bias[: 6 * part_width].reshape(6, part_width)
    qv_bias = head_bias[6 * part_width : 8 * part_width].reshape(2, part_width)
    fc1_bias = head_bias[8 * part_width :]
    silu_all = jax.nn.silu(cond_all).astype(bf16)
    silu_own = lax.dynamic_slice_in_dim(silu_all, dp_index * shard, shard, axis=1)
    mod_terms = jnp.einsum("ld,dke->lke", silu_own, ada_w, preferred_element_type=f32)
    mod_part = plan.tie(plan.reduce_small(mod_terms) + ada_bias, tokens_all[-1])
    modulation = plan.columns(mod_part)
    shift_one, scale_one, gate_two = [modulation[k : k + 1] for k in (0, 1, 5)]

    attn_blocks = []
    for rows in tokens_all:
        normed, _ = normalize(rows.astype(f32))
        attn_blocks.append((normed * (1.0 + scale_one) + shift_one).astype(bf16))
    qkv_full = first_full[:, :qkv_width]
    qkv_bias = jnp.concatenate([qv_bias[0], jnp.zeros((part_width,), f32), qv_bias[1]])
    attn_all = stack_rows(attn_blocks)
    projected = (dot_rows(attn_all, qkv_full) + qkv_bias).astype(bf16)

    proj_full = first_full[:, qkv_width : qkv_width + part_width]
    far_proj = first_full[:, qkv_width + part_width :]
    grad_two = [
        (gate_two * rows.astype(f32)).astype(bf16) for rows in plan.gather(grad_out, grad_out_sent)
    ]
    grad_two_all = stack_rows(grad_two)
    attended = [None] * plan.blocks

    def rows_of(values, block):
        count = values.shape[0] // plan.blocks
        return values[block * count : (block + 1) * count]

    def attend(block, items):
        return attention(items, block, plan.blocks, part_width, head_size)

    def attend_term(block, earlier):
        attended[block] = attend(block, projected)
        return dot_last(attended[block], proj_full)

    if paired:
        attended_sent = plan.send(attend(1, projected))
        attended_own = attend(0, plan.tie(projected, grad_out_sent))
        branch_one = dot_last(attended_own, proj_full) + dot_last(attended_sent, far_proj)
    else:
        branch_one = plan.scatter(attend_term)[0].astype(f32)
    proj_bias = proj_bias.reshape(1, width)
    fc2_bias = fc2_bias.reshape(1, width)
    residual_mid, mlp_low = over_rows(
        middle_kernel, (tokens, branch_one), (proj_bias, modulation), (f32, bf16), False
    )
    mlp_blocks = plan.gather(mlp_low, plan.send(mlp_low))
    mlp_all = stack_rows(mlp_blocks)
    active_blocks = [None] * plan.blocks

    grad_hidden = [None] * plan.blocks

    def mlp_back_term(block, earlier):
        grads, rows = grad_two[block], mlp_blocks[block]
        if earlier is not None:
            grads, rows, _ = plan.hold(grads, rows, earlier)
        hidden = dot_rows(rows, fc1_full) + fc1_bias
        activated, pull = jax.vjp(gelu_tanh, hidden)
        active_blocks[block] = activated.astype(bf16)
        grad_hidden[block] = pull(dot_rows(grads, fc2_full))[0].astype(bf16)
        return dot_last(grad_hidden[block], fc1_full)

    grad_mlp_own, grad_mlp_sent = plan.scatter(mlp_back_term)
    grad_hidden_all = stack_rows(grad_hidden)
    active = stack_rows(active_blocks)
    mlp_sums = lax.dot_general(
        jnp.stack([mlp_all, grad_two_all]),
        jnp.stack([grad_hidden_all, active]),
        (((1,), (1,)), ((0,), (0,))),
        preferred_element_type=f32,
    ).astype(bf16)
    second_sum = lax.psum_scatter(mlp_sums, "dp", scatter_dimension=1, tiled=True)
    grad_mlp_own = plan.tie(grad_mlp_own, mlp_sums)
    grad_resid, grad_branch_one, middle_sums = over_rows(
        middle_back_kernel,
        (residual_mid, branch_one, *plan.pair(grad_mlp_own, grad_mlp_sent), grad_out),
        (proj_bias, modulation),
        (f32, bf16),
        True,
    )
    proj_sum = middle_sums[3]
    grad_proj_sent = None
    if paired:
        far_grads = dot_rows(grad_branch_one, far_proj).astype(bf16)
        grad_attended_sent = plan.send(far_grads)
        grad_attended = dot_rows(grad_branch_one, proj_full).astype(bf16)
        grad_rows = plan.tie(grad_branch_one, far_grads)
        far_proj_sum = dot_first(grad_rows, attended_sent).astype(bf16)
        grad_proj = dot_first(grad_rows, attended_own).astype(bf16)
        grad_attended_sent = plan.tie(grad_attended_sent, far_proj_sum, grad_proj)
        grad_proj_sent = plan.send(plan.tie(far_proj_sum, grad_attended_sent))
        proj_sum = plan.sum_tensor(plan.tie(proj_sum, grad_attended_sent))
        grad_attended = stack_rows([grad_attended, grad_attended_sent])
    else:
        grad_one_all = stack_rows(plan.gather(grad_branch_one, plan.send(grad_branch_one)))
        proj_sum = jnp.sum(grad_one_all, axis=0, dtype=f32)
        grad_proj = dot_first(grad_one_all, stack_rows(attended)).astype(bf16)
        grad_attended = dot_rows(grad_one_all, proj_full).astype(bf16)

    if paired:
        far_rows = dot_last(plan.tie(active_blocks[1], far_grads), fc2_full).astype(bf16)
    else:
        branch_two = plan.scatter(lambda block, e: dot_last(active_blocks[0], fc2_full))[0]
        branch_two_parts = plan.pair(branch_two, None)

    def token_sum(values):
        return jnp.sum(values, axis=0, dtype=f32)

    head_sums = sum(token_sum(v) for v in grad_hidden)
    if paired:
        head_sums, grad_attended = plan.hold(head_sums, grad_attended)
    head_sums = head_sums.reshape(-1, dp_size, piece).transpose(1, 0, 2).reshape(dp_size, -1)
    bias_sums = jnp.concatenate(
        [
            head_sums,
            proj_sum.reshape(dp_size, shard),
            token_sum(grad_two_all).reshape(dp_size, shard),
        ],
        axis=1,
    ).astype(bf16)
    bias_sums = jnp.pad(bias_sums, ((0, 0), (0, shard * extra - bias_sums.shape[1])))
    bias_sums = bias_sums.reshape(width, extra)
    lane_blocks = part_width // min(128, part_width)
    calls = 2 if lane_blocks % 2 == 0 else 1
    grad_projected = None
    for call in range(calls):
        if call == 1 and paired:
            grad_attended, grad_proj_sent, bias_sums, grad_projected, far_rows = plan.hold(
                grad_attended, grad_proj_sent, bias_sums, grad_projected, far_rows
            )
            branch_two_sent = plan.send(far_rows)
        grad_projected = attention_back(
            projected,
            grad_attended,
            grad_projected,
            call * (lane_blocks // calls),
            lane_blocks // calls,
            part_width,
            head_size,
        )

    def attn_back_term(block, earlier):
        items = rows_of(grad_projected, block)
        if earlier is not None:
            items = plan.tie(items, earlier)
        return dot_last(items, qkv_full)

    if paired:
        branch_two_sent, grad_projected = plan.hold(branch_two_sent, grad_projected)
    grad_attn_own, grad_attn_sent = plan.scatter(attn_back_term)
    if paired:
        own_active, grad_attn_own = plan.hold(active_blocks[0], grad_attn_own)
        branch_two_parts = (dot_last(own_active, fc2_full), branch_two_sent)
    block_out, last_sums = over_rows(
        finish_kernel,
        (residual_mid, *branch_two_parts, grad_out),
        (fc2_bias, modulation),
        (bf16,),
        True,
    )
    grad_attn_own, grad_projected, block_out, last_sums = plan.hold(
        grad_attn_own, grad_projected, block_out, last_sums
    )
    qkv_sums = token_sum(grad_projected)
    qv_sums = jnp.stack([qkv_sums[:part_width], qkv_sums[2 * part_width :]]).astype(bf16)
    first_sum = dot_first(attn_all, grad_projected).astype(bf16)
    if paired:
        grad_proj = plan.add(grad_proj, grad_proj_sent)
    first_sum = jnp.concatenate([first_sum, grad_proj, bias_sums], axis=1)
    if paired:
        first_sum = first_sum.reshape((2, 2, 2, 2, shard, -1))
        half = first_sum.shape[-1] // 256 * 128
        first_sum, grad_attn_sent, qv_sums = plan.hold(first_sum, grad_attn_sent, qv_sums)
        held, received = plan.step(first_sum, 1, 3)
        first_sum = plan.add(held, received)
        one = plan.step(first_sum[..., :half], 2, 2)
        two = plan.step(first_sum[..., half:], 4, 1)
    else:
        first_sum = plan.scatter_last(first_sum)
    grad_tokens, first_sums = over_rows(
        first_back_kernel,
        (tokens, *plan.pair(grad_attn_own, grad_attn_sent), grad_resid),
        (modulation,),
        (bf16,),
        True,
    )
    sums = jnp.concatenate([first_sums[:2], middle_sums[:3], last_sums[:1]], axis=0)
    grad_mod = plan.scatter_columns(sums).astype(bf16)
    grad_mod, second_sum = plan.hold(grad_mod, second_sum)
    grad_mod = plan.gather_dp(jnp.concatenate([grad_mod, qv_sums], axis=0))
    qv_sums = jnp.sum(grad_mod[:, 6:], axis=0, dtype=f32).reshape(2, heads_part, head_size)
    grad_qv_b = lax.dynamic_slice_in_dim(qv_sums, dp_index * piece, piece, axis=2)
    grad_mod = grad_mod[:, :6]
    if paired:
        one_sent, two_sent, grad_mod = plan.hold(one[1], two[1], grad_mod)
        one = plan.step(plan.add(one[0], one_sent), 4, 1)
        two = plan.step(plan.add(two[0], two_sent), 8, 0)
    grad_silu = jnp.einsum("lke,dke->ld", grad_mod, ada_w, preferred_element_type=f32)
    grad_silu = plan.sum_tensor(grad_silu)
    if paired:
        one_sent, two_sent, grad_silu = plan.hold(one[1], two[1], grad_silu)
        one = plan.step(plan.add(one[0], one_sent), 8, 0)
        two = plan.step(plan.add(two[0], two_sent), 2, 0)
    grad_silu = plan.gather_dp(grad_silu)
    if paired:
        first_sum = jnp.concatenate([plan.add(*one), plan.add(*two)], axis=-1)
    grad_ada_w = jnp.einsum("ld,lke->dke", silu_own, grad_mod, preferred_element_type=f32)
    grad_ada_b = jnp.sum(grad_mod, axis=0, dtype=f32).reshape(6, heads_part, head_size)
    grad_ada_b = lax.dynamic_slice_in_dim(grad_ada_b, dp_index * piece, piece, axis=2)
    grad_silu = lax.dynamic_index_in_dim(grad_silu, dp_index, 1, keepdims=False).reshape(1, width)
    grad_cond = jax.vjp(jax.nn.silu, cond.astype(f32))[1](grad_silu)[0].astype(bf16)

    owned = first_sum[:, qkv_width + part_width :].reshape(-1).astype(f32)
    start = fc1_b.size
    grad_fc1_b = owned[:start].reshape(fc1_b.shape)
    return (
        block_out,
        grad_tokens,
        grad_cond,
        grad_ada_w,
        grad_ada_b,
        first_sum[:, :qkv_width].astype(f32).reshape(qkv_w.shape),
        grad_qv_b,
        first_sum[:, qkv_width : qkv_width + part_width].astype(f32).T,
        owned[start : start + shard],
        second_sum[0].astype(f32),
        grad_fc1_b,
        second_sum[1].astype(f32).T,
        owned[start + shard : start + 2 * shard],
    )


def solution(mesh):
    rows = P(("dp", "tensor"), None)
    ada = P("dp", None, "tensor")
    heads = P(None, "tensor", "dp")
    out = P("tensor", "dp")
    weights = (ada, heads, ada, heads, out, P("dp"), P("dp", "tensor"), out, out, P("dp"))
    return jax.shard_map(
        functools.partial(body, mesh.shape["dp"], mesh.shape["tensor"]),
        mesh=mesh,
        in_specs=(rows, P("dp", None)) + weights + (rows,),
        out_specs=(rows, rows, P("dp", None)) + weights,
        check_vma=False,
    )
```
